256 devices in a mesh: fsdp: 16 (over z, core), slab: 8 (over y, x_lo), rep: 2 (over x_hi).
Axes of the slice: x: 4 (x_hi: 2, x_lo: 2; x = x_hi * 2 + x_lo), y: 4, z: 8, core: 2. Of those that a mesh axis runs over, the one named last changes fastest.
Arguments:
- inputs: bfloat16 [32, 32, 8, 8, 256], P(('fsdp', 'rep'), 'slab'), may hold values from -6 to 6
- weights: bfloat16 [256, 27, 256], P('fsdp'), may hold values from -0.078125 to 0.078125
- upstream: bfloat16 [32, 32, 8, 8, 256], P(('fsdp', 'rep'), 'slab'), may hold values from -6 to 6
Outputs:
- activated: bfloat16 [32, 32, 8, 8, 256], P(('fsdp', 'rep'), 'slab')
- input_grad: bfloat16 [32, 32, 8, 8, 256], P(('fsdp', 'rep'), 'slab')
- weight_grad: float32 [256, 27, 256], P('fsdp')
The draws below stay inside these ranges and needn't reach their ends.
All inputs are finite; a program needn't handle non-finite values.
Results may differ from the reference program's by a relative error of at most 0.0049.
Values may be sent and summed in bfloat16 or wider, within the bound.
No kernel may reach another device: no remote copies, remote signals or barrier semaphores. Data moves between devices by JAX's collectives and lax.ppermute only.
A program may use at most 256 MiB of HBM per device.

```python
import jax
import jax.numpy as jnp

CIN = 256
COUT = 256
TAPS = 27
GY = 8
GZ = 8
BATCH = 32
NX = 32


def strengthened(entries, key, source, target, parts, factor):
    owner, partner = [(jnp.arange(entries.shape[dim]) // (entries.shape[dim] // parts)).reshape([-1 if axis == dim else 1 for axis in range(entries.ndim)]) for dim in (source, target)]
    chosen = jax.random.permutation(key, parts)[partner]
    strong = (owner == chosen) | (owner == (partner + parts // 2) % parts)
    return jnp.where(strong, factor * entries, entries)


def levels(own_key, shape, split, low, high):
    factor_of, own = 1.0, jax.random.fold_in(own_key, 6)
    for position, parts in split:
        draws = jnp.exp(jax.random.uniform(jax.random.fold_in(own, position), (parts,), jnp.float32, low / len(split), high / len(split)))
        factor_of = factor_of * jnp.repeat(draws, shape[position] // parts).reshape([-1 if axis == position else 1 for axis in range(len(shape))])
    return factor_of


def centred(key, shape, scale, bound, split=(), kind=jnp.bfloat16):
    result = jax.random.normal(key, shape, jnp.float32) * scale
    if len(split) > 0:
        result = levels(key, shape, split, -0.22, 0.18) * result
    return jnp.clip(result, min=-bound, max=bound).astype(kind)


def gaussian_with(key, dims, scale, reach, cuts, heavy, kind=jnp.bfloat16):
    values = scale * jax.random.normal(key, dims, jnp.float32)
    if cuts:
        values = values * levels(key, dims, cuts, -0.22, 0.18)
    return jnp.clip(strengthened(values, jax.random.fold_in(key, 3), *heavy), -reach, reach).astype(kind)


def setup_inputs(seed: int = 0) -> dict:
    splits = jax.random.split(jax.random.key(seed), 4)
    return {
        "inputs": centred(splits[0], (BATCH, NX, GY, GZ, CIN), 1.0, 6.0, ((0, 32), (1, 8))),
        "weights": centred(splits[1], (COUT, TAPS, CIN), (TAPS * CIN) ** -0.5, 0.078125, ((0, 16),)),
        "upstream": gaussian_with(splits[2], (BATCH, NX, GY, GZ, COUT), 1.0, 6.0, ((0, 32), (1, 8)), (0, 4, 32, 2.75)),
    }


def tap_list():
    return [(along_x, along_y, along_z) for along_x in range(3) for along_y in range(3) for along_z in range(3)]


def silu_slope(preact):
    logistic = jax.nn.sigmoid(preact)
    return logistic * (1.0 + preact * (1.0 - logistic))


def pad_grid(field):
    return jnp.pad(field, ((0, 0), (1, 1), (1, 1), (1, 1), (0, 0)))


def reference(inputs, weights, upstream):
    planes = inputs.shape[1]
    height = inputs.shape[2]
    breadth = inputs.shape[3]
    padded = pad_grid(inputs)
    preact = jnp.zeros(upstream.shape, jnp.float32)
    for index, (along_x, along_y, along_z) in enumerate(tap_list()):
        window = padded[:, along_x:along_x + planes, along_y:along_y + height, along_z:along_z + breadth, :].astype(jnp.float32)
        preact = preact + jnp.einsum("bxyzi,oi->bxyzo", window, weights[:, index, :].astype(jnp.float32))
    activated = jax.nn.silu(preact).astype(jnp.bfloat16)
    grad_pre = (upstream.astype(jnp.float32) * silu_slope(preact)).astype(jnp.bfloat16)
    grads_pad = pad_grid(grad_pre)
    grad_wide = grad_pre.astype(jnp.float32)
    input_sum = jnp.zeros(inputs.shape, jnp.float32)
    tap_grads = []
    for index, (along_x, along_y, along_z) in enumerate(tap_list()):
        grad_window = grads_pad[:, 2 - along_x:2 - along_x + planes, 2 - along_y:2 - along_y + height, 2 - along_z:2 - along_z + breadth, :].astype(jnp.float32)
        input_sum = input_sum + jnp.einsum("bxyzo,oi->bxyzi", grad_window, weights[:, index, :].astype(jnp.float32))
        window = padded[:, along_x:along_x + planes, along_y:along_y + height, along_z:along_z + breadth, :].astype(jnp.float32)
        tap_grads.append(jnp.einsum("bxyzo,bxyzi->oi", grad_wide, window))
    factor = float(BATCH * NX * GY * GZ) ** -0.5
    weight_grad = jnp.stack(tap_grads, axis=1) * factor
    return activated, input_sum.astype(jnp.bfloat16), weight_grad
```

```python
import functools

import jax
import jax.numpy as jnp
from jax import lax
from jax.experimental import pallas as pl
from jax.experimental.pallas import tpu as pltpu
from jax.sharding import PartitionSpec as P

F32 = jnp.float32
BF16 = jnp.bfloat16
CELLS = 256
LANES = 128
SLABS = 8
OUTS = 32
TAPS = 27
ROWS = 28 * OUTS
WHOLE = SLABS * CELLS
COLUMNS = WHOLE // LANES


def tap_index(along_x, along_y, along_z):
    return (along_x * 3 + along_y) * 3 + along_z


def pack_kernel(x_ref, u_ref, out_ref):
    turned = jnp.transpose(u_ref[...].astype(F32)).astype(BF16)
    for slab in range(SLABS):
        out_ref[slab, :CELLS, :] = x_ref[...]
        out_ref[slab, CELLS:, :] = turned[slab * OUTS : (slab + 1) * OUTS]


def lane_masks():
    lane = lax.broadcasted_iota(jnp.int32, (16, LANES), 1)
    row = (lane >> 3) & 7
    col = lane & 7
    return lane < 64, row, col


def inside(coordinate, shift):
    moved = coordinate + shift
    return (moved >= 0) & (moved < 8)


def turn(block, shift):
    return pltpu.roll(block, shift % LANES, 1)


def main_kernel(core_ref, r_ref, w_ref, act_ref, own_ref, other_ref, g_ref, w2_ref, z_ref):
    for tap in range(TAPS):
        for core in range(2):
            w2_ref[tap * OUTS + core * 16 : tap * OUTS + core * 16 + 16, :] = w_ref[
                (tap // 4) * 2 + core, (tap % 4) * 16 : (tap % 4) * 16 + 16, :
            ]
    w2_ref[TAPS * OUTS :, :] = jnp.zeros((OUTS, CELLS), BF16)
    g_ref[TAPS * OUTS :, :] = jnp.zeros((OUTS, WHOLE), BF16)
    taps_by_outs = w2_ref[: TAPS * OUTS, :]
    for slab in range(SLABS):
        z_ref[:, slab * CELLS : (slab + 1) * CELLS] = lax.dot_general(
            taps_by_outs,
            r_ref[slab, :CELLS, :],
            (((1,), (1,)), ((), ())),
            preferred_element_type=F32,
        )
    low, row, col = lane_masks()
    zero = jnp.zeros((16, LANES), F32)
    for group in range(2):

        def term(along_x, along_y, along_z, column):
            if column < 0 or column >= COLUMNS:
                return zero
            start = tap_index(along_x, along_y, along_z) * OUTS + group * 16
            return z_ref[start : start + 16, column * LANES : (column + 1) * LANES]

        grads = []
        for column in range(COLUMNS):
            total = None
            for c in range(3):
                over_y = None
                for b in range(3):
                    mixed = jnp.where(
                        low,
                        term(2, b, c, column + 1) + term(0, b, c, column),
                        term(2, b, c, column) + term(0, b, c, column - 1),
                    )
                    over_x = term(1, b, c, column) + turn(mixed, 64)
                    if b != 1:
                        over_x = jnp.where(inside(row, b - 1), turn(over_x, -8 * (b - 1)), 0.0)
                    over_y = over_x if over_y is None else over_y + over_x
                if c != 1:
                    over_y = jnp.where(inside(col, c - 1), turn(over_y, -(c - 1)), 0.0)
                total = over_y if total is None else total + over_y
            slab, part = column // 2, column % 2
            lanes = slice(part * LANES, (part + 1) * LANES)
            outs = slice(group * 16, group * 16 + 16)
            logistic = 1.0 / (1.0 + jnp.exp(-total))
            act_ref[slab, outs, lanes] = (total * logistic).astype(BF16)
            upstream = r_ref[
                slab, CELLS + group * 16 : CELLS + group * 16 + 16, lanes
            ].astype(F32)
            grad = upstream * (logistic * (1.0 + total * (1.0 - logistic)))
            grads.append(grad.astype(BF16).astype(F32))
        for c in range(3):
            if c == 1:
                by_z = grads
            else:
                by_z = [jnp.where(inside(col, 1 - c), turn(g, c - 1), 0.0) for g in grads]
            for b in range(3):
                if b == 1:
                    by_y = by_z
                else:
                    by_y = [
                        jnp.where(inside(row, 1 - b), turn(g, 8 * (b - 1)), 0.0) for g in by_z
                    ]
                swapped = [zero] + [turn(g, 64) for g in by_y] + [zero]
                for column in range(COLUMNS):
                    lanes = slice(column * LANES, (column + 1) * LANES)
                    here = swapped[column + 1]
                    for a, value in (
                        (0, jnp.where(low, here, swapped[column + 2])),
                        (1, by_y[column]),
                        (2, jnp.where(low, swapped[column], here)),
                    ):
                        start = tap_index(a, b, c) * OUTS + group * 16
                        g_ref[start : start + 16, lanes] = value.astype(BF16)
    whole = jnp.dot(
        g_ref[: TAPS * OUTS, :],
        r_ref[:, :CELLS, :].reshape(WHOLE, CELLS),
        preferred_element_type=F32,
    )
    first = core_ref[0] == 0
    for tap in range(TAPS):
        start = tap * OUTS
        left = whole[start : start + 16]
        right = whole[start + 16 : start + 32]
        own_ref[tap * 16 : tap * 16 + 16, :] = jnp.where(first, left, right)
        other_ref[tap * 16 : tap * 16 + 16, :] = jnp.where(first, right, left).astype(
            other_ref.dtype
        )
    own_ref[TAPS * 16 :, :] = jnp.zeros((5 * 16, CELLS), own_ref.dtype)
    other_ref[TAPS * 16 :, :] = jnp.zeros((5 * 16, CELLS), other_ref.dtype)


def input_kernel(g_ref, w2_ref, act_ref, out_ref):
    turned = jnp.transpose(w2_ref[...].astype(F32)).astype(BF16)
    for slab in range(SLABS):
        out_ref[slab, :CELLS, :] = jnp.dot(
            turned, g_ref[:, slab * CELLS : (slab + 1) * CELLS], preferred_element_type=F32
        ).astype(BF16)
        out_ref[slab, CELLS:, :] = act_ref[slab]


def final_kernel(r_ref, act_ref, grad_ref):
    total = r_ref[0, :CELLS, :].astype(F32)
    for slab in range(1, SLABS):
        total = total + r_ref[slab, :CELLS, :].astype(F32)
    grad_ref[...] = jnp.transpose(total).astype(BF16)
    act_ref[...] = jnp.transpose(r_ref[:, CELLS:, :].astype(F32).reshape(CELLS, CELLS)).astype(BF16)


VMEM = pl.BlockSpec(memory_space=pltpu.VMEM)
SMEM = pl.BlockSpec(memory_space=pltpu.SMEM)
PARAMS = pltpu.CompilerParams(vmem_limit_bytes=48 * 1024 * 1024)


def shape(*dims, dtype=BF16):
    return jax.ShapeDtypeStruct(dims, dtype)


def call(kernel, outs, operands, specs=None, scratch=(), flops=0):
    moved = sum(a.size * a.dtype.itemsize for a in list(operands) + list(outs))
    return pl.pallas_call(
        kernel,
        out_shape=tuple(outs),
        in_specs=specs or [VMEM] * len(operands),
        out_specs=tuple(VMEM for _ in outs),
        scratch_shapes=list(scratch),
        compiler_params=PARAMS,
        cost_estimate=pl.CostEstimate(flops=flops, bytes_accessed=moved, transcendentals=0),
    )(*operands)


def repeated(block, count):
    return jnp.broadcast_to(block[None], (count,) + block.shape)


def local(inputs, weights, upstream):
    owner = lax.axis_index("fsdp")
    slab = lax.axis_index("slab")
    chips = lax.axis_size("fsdp") // 2
    reps = lax.axis_size("rep")
    total_cells = 2 * chips * reps * WHOLE
    factor = float(total_cells) ** (-0.5)

    def place(z, core, y, rep):
        return ((z * 2 + core) * SLABS + y) * reps + rep

    everyone = ("fsdp", "slab", "rep")
    crossed = [
        (place(z, core, y, rep), place(y, core, z, rep))
        for z in range(chips)
        for core in range(2)
        for y in range(SLABS)
        for rep in range(reps)
    ]
    cores = [(2 * z + core, 2 * z + 1 - core) for z in range(chips) for core in range(2)]
    columns = [[2 * z + core for z in range(chips)] for core in range(2)]

    by_tap = jnp.pad(jnp.transpose(weights, (1, 0, 2)), ((0, 5), (0, 0), (0, 0)))
    piece = lax.dynamic_slice_in_dim(by_tap, slab * 4, 4, axis=0).reshape(64, CELLS)
    piece = lax.ppermute(piece, everyone, crossed)
    pieces = lax.all_to_all(repeated(piece, 2 * chips), "fsdp", 0, 0)

    cells = inputs.reshape(CELLS, CELLS)
    packed = call(
        pack_kernel,
        [shape(SLABS, CELLS + OUTS, CELLS)],
        (cells, upstream.reshape(CELLS, CELLS)),
    )[0]
    gathered = lax.all_to_all(packed, "slab", 0, 0)

    core = (owner % 2).astype(jnp.int32).reshape(1)
    act, own, other, grads, kernel_rows = call(
        main_kernel,
        [
            shape(SLABS, OUTS, CELLS),
            shape(512, CELLS, dtype=F32),
            shape(512, CELLS, dtype=F32),
            shape(ROWS, WHOLE),
            shape(ROWS, CELLS),
        ],
        (core, gathered, pieces),
        specs=[SMEM, VMEM, VMEM],
        scratch=[pltpu.VMEM((TAPS * OUTS, WHOLE), F32)],
        flops=4 * ROWS * WHOLE * CELLS,
    )
    own = own + lax.ppermute(other, "fsdp", cores)
    sums = lax.all_to_all(
        own.astype(BF16).reshape(chips, 64, CELLS), "fsdp", 0, 0, axis_index_groups=columns
    )
    sums = jnp.sum(sums.astype(F32), axis=0).astype(BF16)

    terms = call(
        input_kernel,
        [shape(SLABS, CELLS + OUTS, CELLS)],
        (grads, kernel_rows, act),
        flops=2 * ROWS * WHOLE * CELLS,
    )[0]
    returned = lax.all_to_all(terms, "slab", 0, 0)
    activated, input_grad = call(
        final_kernel, [shape(CELLS, CELLS), shape(CELLS, CELLS)], (returned,)
    )

    sums = lax.ppermute(sums, everyone, crossed)
    parts = lax.all_to_all(repeated(sums, SLABS * reps), ("slab", "rep"), 0, 0)
    parts = jnp.sum(parts.reshape(SLABS, reps, 64, CELLS).astype(F32), axis=1)
    weight_grad = jnp.transpose(parts.reshape(32, 16, CELLS)[:TAPS], (1, 0, 2)) * factor
    return (
        activated.reshape(inputs.shape),
        input_grad.reshape(inputs.shape),
        weight_grad,
    )


def solution(mesh):
    placed = (
        P(("fsdp", "rep"), "slab", None, None, None),
        P("fsdp", None, None),
        P(("fsdp", "rep"), "slab", None, None, None),
    )
    return jax.shard_map(
        local,
        mesh=mesh,
        in_specs=placed,
        out_specs=(
            P(("fsdp", "rep"), "slab", None, None, None),
            P(("fsdp", "rep"), "slab", None, None, None),
            P("fsdp", None, None),
        ),
        check_vma=False,
    )
```

```python
import jax
import jax.numpy as jnp
from jax import lax
from jax.experimental import pallas as pl
from jax.experimental.pallas import tpu as pltpu
from jax.sharding import PartitionSpec as P

F32 = jnp.float32
BF16 = jnp.bfloat16
CELLS = 256
LANES = 128
SLABS = 8
OUTS = 32
TAPS = 27
ROWS = 28 * OUTS
WHOLE = SLABS * CELLS
COLUMNS = WHOLE // LANES


def tap_index(along_x, along_y, along_z):
    return (along_x * 3 + along_y) * 3 + along_z


def pack_kernel(x_ref, u_ref, out_ref):
    turned = jnp.transpose(u_ref[...].astype(F32)).astype(BF16)
    for slab in range(SLABS):
        out_ref[slab, :CELLS, :] = x_ref[...]
        out_ref[slab, CELLS:, :] = turned[slab * OUTS : (slab + 1) * OUTS]


def lane_masks():
    lane = lax.broadcasted_iota(jnp.int32, (16, LANES), 1)
    row = (lane >> 3) & 7
    col = lane & 7
    return lane < 64, row, col


def inside(coordinate, shift):
    moved = coordinate + shift
    return (moved >= 0) & (moved < 8)


def turn(block, shift):
    return pltpu.roll(block, shift % LANES, 1)


def main_kernel(
    core_ref, r_ref, same_ref, opposite_ref, out_ref, own_ref, other_ref, g_ref, w2_ref, z_ref
):
    first = core_ref[0] == 0
    for tap in range(TAPS):
        start = tap * OUTS
        same, opposite = same_ref[tap], opposite_ref[tap]
        w2_ref[start : start + 16, :] = jnp.where(first, same, opposite)
        w2_ref[start + 16 : start + 32, :] = jnp.where(first, opposite, same)
    w2_ref[TAPS * OUTS :, :] = jnp.zeros((OUTS, CELLS), BF16)
    g_ref[TAPS * OUTS :, :] = jnp.zeros((OUTS, WHOLE), BF16)
    taps_by_outs = w2_ref[: TAPS * OUTS, :]
    for slab in range(SLABS):
        z_ref[:, slab * CELLS : (slab + 1) * CELLS] = lax.dot_general(
            taps_by_outs,
            r_ref[slab, :CELLS, :],
            (((1,), (1,)), ((), ())),
            preferred_element_type=F32,
        )
    low, row, col = lane_masks()
    zero = jnp.zeros((16, LANES), F32)
    for group in range(2):

        def term(along_x, along_y, along_z, column):
            if column < 0 or column >= COLUMNS:
                return zero
            start = tap_index(along_x, along_y, along_z) * OUTS + group * 16
            return z_ref[start : start + 16, column * LANES : (column + 1) * LANES]

        grads = []
        for column in range(COLUMNS):
            total = None
            for c in range(3):
                over_y = None
                for b in range(3):
                    mixed = jnp.where(
                        low,
                        term(2, b, c, column + 1) + term(0, b, c, column),
                        term(2, b, c, column) + term(0, b, c, column - 1),
                    )
                    over_x = term(1, b, c, column) + turn(mixed, 64)
                    if b != 1:
                        over_x = jnp.where(inside(row, b - 1), turn(over_x, -8 * (b - 1)), 0.0)
                    over_y = over_x if over_y is None else over_y + over_x
                if c != 1:
                    over_y = jnp.where(inside(col, c - 1), turn(over_y, -(c - 1)), 0.0)
                total = over_y if total is None else total + over_y
            slab, part = column // 2, column % 2
            lanes = slice(part * LANES, (part + 1) * LANES)
            logistic = 1.0 / (1.0 + jnp.exp(-total))
            out_ref[slab, CELLS + group * 16 : CELLS + group * 16 + 16, lanes] = (
                total * logistic
            ).astype(BF16)
            upstream = r_ref[
                slab, CELLS + group * 16 : CELLS + group * 16 + 16, lanes
            ].astype(F32)
            grad = upstream * (logistic * (1.0 + total * (1.0 - logistic)))
            grads.append(grad.astype(BF16).astype(F32))
        for c in range(3):
            if c == 1:
                by_z = grads
            else:
                by_z = [jnp.where(inside(col, 1 - c), turn(g, c - 1), 0.0) for g in grads]
            for b in range(3):
                if b == 1:
                    by_y = by_z
                else:
                    by_y = [
                        jnp.where(inside(row, 1 - b), turn(g, 8 * (b - 1)), 0.0) for g in by_z
                    ]
                swapped = [zero] + [turn(g, 64) for g in by_y] + [zero]
                for column in range(COLUMNS):
                    lanes = slice(column * LANES, (column + 1) * LANES)
                    here = swapped[column + 1]
                    for a, value in (
                        (0, jnp.where(low, here, swapped[column + 2])),
                        (1, by_y[column]),
                        (2, jnp.where(low, swapped[column], here)),
                    ):
                        start = tap_index(a, b, c) * OUTS + group * 16
                        g_ref[start : start + 16, lanes] = value.astype(BF16)
    whole = jnp.dot(
        g_ref[: TAPS * OUTS, :],
        r_ref[:, :CELLS, :].reshape(WHOLE, CELLS),
        preferred_element_type=F32,
    )
    for tap in range(TAPS):
        start = tap * OUTS
        left = whole[start : start + 16]
        right = whole[start + 16 : start + 32]
        own_ref[tap * 16 : tap * 16 + 16, :] = jnp.where(first, left, right)
        other_ref[tap * 16 : tap * 16 + 16, :] = jnp.where(first, right, left).astype(
            other_ref.dtype
        )
    own_ref[TAPS * 16 :, :] = jnp.zeros((5 * 16, CELLS), own_ref.dtype)
    other_ref[TAPS * 16 :, :] = jnp.zeros((5 * 16, CELLS), other_ref.dtype)
    turned = jnp.transpose(w2_ref[...].astype(F32)).astype(BF16)
    for slab in range(SLABS):
        out_ref[slab, :CELLS, :] = jnp.dot(
            turned, g_ref[:, slab * CELLS : (slab + 1) * CELLS], preferred_element_type=F32
        ).astype(BF16)


def halve_kernel(bit_ref, mine_ref, got_ref, kept_ref, sent_ref):
    half = kept_ref.shape[0]
    total = mine_ref[...] + got_ref[...].astype(F32)
    first = bit_ref[0] == 0
    kept_ref[...] = jnp.where(first, total[:half], total[half:])
    sent_ref[...] = jnp.where(first, total[half:], total[:half]).astype(BF16)


def share_kernel(left_ref, right_ref, after_ref, out_ref):
    total = (left_ref[...].astype(F32) + right_ref[...].astype(F32)).astype(BF16)
    for slab in range(SLABS):
        out_ref[slab] = total


def final_kernel(r_ref, act_ref, grad_ref):
    total = r_ref[0, :CELLS, :].astype(F32)
    for slab in range(1, SLABS):
        total = total + r_ref[slab, :CELLS, :].astype(F32)
    grad_ref[...] = jnp.transpose(total).astype(BF16)
    act_ref[...] = jnp.transpose(r_ref[:, CELLS:, :].astype(F32).reshape(CELLS, CELLS)).astype(BF16)


VMEM = pl.BlockSpec(memory_space=pltpu.VMEM)
SMEM = pl.BlockSpec(memory_space=pltpu.SMEM)
PARAMS = pltpu.CompilerParams(vmem_limit_bytes=48 * 1024 * 1024)


def shape(*dims, dtype=BF16):
    return jax.ShapeDtypeStruct(dims, dtype)


def call(kernel, outs, operands, specs=None, scratch=(), flops=0):
    moved = sum(a.size * a.dtype.itemsize for a in list(operands) + list(outs))
    return pl.pallas_call(
        kernel,
        out_shape=tuple(outs),
        in_specs=specs or [VMEM] * len(operands),
        out_specs=tuple(VMEM for _ in outs),
        scratch_shapes=list(scratch),
        compiler_params=PARAMS,
        cost_estimate=pl.CostEstimate(flops=flops, bytes_accessed=moved, transcendentals=0),
    )(*operands)


def reversed_bits(z):
    return (z & 1) * 4 + (z & 2) + (z >> 2)


def local(inputs, weights, upstream):
    owner = lax.axis_index("fsdp")
    slab = lax.axis_index("slab")
    chips = lax.axis_size("fsdp") // 2
    reps = lax.axis_size("rep")
    total_cells = 2 * chips * reps * WHOLE
    factor = float(total_cells) ** (-0.5)

    def place(z, core, y, rep):
        return ((z * 2 + core) * SLABS + y) * reps + rep

    everyone = ("fsdp", "slab", "rep")
    crossed = [
        (place(z, core, y, rep), place(y, core, z, rep))
        for z in range(chips)
        for core in range(2)
        for y in range(SLABS)
        for rep in range(reps)
    ]
    cores = [(2 * z + core, 2 * z + 1 - core) for z in range(chips) for core in range(2)]

    by_tap = jnp.transpose(weights, (1, 0, 2))
    same = lax.ppermute(by_tap, everyone, crossed)
    opposite = lax.ppermute(same, "fsdp", cores)

    cells = inputs.reshape(CELLS, CELLS)
    packed = call(
        pack_kernel,
        [shape(SLABS, CELLS + OUTS, CELLS)],
        (cells, upstream.reshape(CELLS, CELLS)),
    )[0]
    gathered = lax.all_to_all(packed, "slab", 0, 0)

    core = (owner % 2).astype(jnp.int32).reshape(1)
    terms, own, other = call(
        main_kernel,
        [
            shape(SLABS, CELLS + OUTS, CELLS),
            shape(512, CELLS, dtype=F32),
            shape(512, CELLS, dtype=F32),
        ],
        (core, gathered, same, opposite),
        specs=[SMEM, VMEM, VMEM, VMEM],
        scratch=[
            pltpu.VMEM((ROWS, WHOLE), BF16),
            pltpu.VMEM((ROWS, CELLS), BF16),
            pltpu.VMEM((TAPS * OUTS, WHOLE), F32),
        ],
        flops=6 * ROWS * WHOLE * CELLS,
    )
    returned = lax.all_to_all(terms, "slab", 0, 0)
    activated, input_grad = call(
        final_kernel, [shape(CELLS, CELLS), shape(CELLS, CELLS)], (returned,)
    )

    got = lax.ppermute(other, "fsdp", cores)
    chip = owner // 2
    for step in range(3):
        bit = ((chip >> step) & 1).astype(jnp.int32).reshape(1)
        half = own.shape[0] // 2
        own, sent = call(
            halve_kernel,
            [shape(half, CELLS, dtype=F32), shape(half, CELLS)],
            (bit, own, got),
            specs=[SMEM, VMEM, VMEM],
        )
        pairs = [
            (2 * z + core, 2 * (z ^ (1 << step)) + core) for z in range(chips) for core in range(2)
        ]
        got = lax.ppermute(sent, "fsdp", pairs)
    sums = (own + got.astype(F32)).astype(BF16)
    shares = [
        lax.ppermute(
            sums,
            everyone,
            [
                (place(z, core, y, rep), place(y, core, reversed_bits(z), (rep + turn_by) % reps))
                for z in range(chips)
                for core in range(2)
                for y in range(SLABS)
                for rep in range(reps)
            ],
        )
        for turn_by in range(reps)
    ]
    share = call(
        share_kernel,
        [shape(SLABS, 64, CELLS)],
        (*shares, returned),
        specs=[VMEM, VMEM, pl.BlockSpec(memory_space=pl.ANY)],
    )[0]
    parts = lax.all_to_all(share, "slab", 0, 0).astype(F32)
    weight_grad = jnp.transpose(parts.reshape(32, 16, CELLS)[:TAPS], (1, 0, 2)) * factor
    return (
        activated.reshape(inputs.shape),
        input_grad.reshape(inputs.shape),
        weight_grad,
    )


def solution(mesh):
    placed = (
        P(("fsdp", "rep"), "slab", None, None, None),
        P("fsdp", None, None),
        P(("fsdp", "rep"), "slab", None, None, None),
    )
    return jax.shard_map(
        local,
        mesh=mesh,
        in_specs=placed,
        out_specs=(
            P(("fsdp", "rep"), "slab", None, None, None),
            P(("fsdp", "rep"), "slab", None, None, None),
            P("fsdp", None, None),
        ),
        check_vma=False,
    )
```

```python
import jax
import jax.numpy as jnp
from jax import lax
from jax.experimental import pallas as pl
from jax.experimental.pallas import tpu as pltpu
from jax.sharding import PartitionSpec as P

F32 = jnp.float32
BF16 = jnp.bfloat16
CELLS = 256
LANES = 128
SLABS = 8
OUTS = 32
TAPS = 27
ROWS = 28 * OUTS
WHOLE = SLABS * CELLS
COLUMNS = WHOLE // LANES


def tap_index(along_x, along_y, along_z):
    return (along_x * 3 + along_y) * 3 + along_z


def pack_kernel(chip_ref, x_ref, u_ref, out_ref):
    turned = jnp.transpose(u_ref[...].astype(F32)).astype(BF16)
    for slab in range(SLABS):
        out_ref[slab, :CELLS, :] = x_ref[...]
    for pair in range(SLABS):
        out_ref[(pair + chip_ref[0]) & 7, CELLS:, :] = turned[pair * OUTS : (pair + 1) * OUTS]


def lane_masks():
    lane = lax.broadcasted_iota(jnp.int32, (16, LANES), 1)
    row = (lane >> 3) & 7
    col = lane & 7
    return lane < 64, row, col


def inside(coordinate, shift):
    moved = coordinate + shift
    return (moved >= 0) & (moved < 8)


def turn(block, shift):
    return pltpu.roll(block, shift % LANES, 1)


def main_kernel(
    core_ref, r_ref, same_ref, opposite_ref, out_ref, own_ref, other_ref, g_ref, w2_ref, z_ref
):
    first = core_ref[0] == 0
    for tap in range(TAPS):
        start = tap * OUTS
        same, opposite = same_ref[tap], opposite_ref[tap]
        w2_ref[start : start + 16, :] = jnp.where(first, same, opposite)
        w2_ref[start + 16 : start + 32, :] = jnp.where(first, opposite, same)
    w2_ref[TAPS * OUTS :, :] = jnp.zeros((OUTS, CELLS), BF16)
    g_ref[TAPS * OUTS :, :] = jnp.zeros((OUTS, WHOLE), BF16)
    taps_by_outs = w2_ref[: TAPS * OUTS, :]
    for slab in range(SLABS):
        z_ref[:, slab * CELLS : (slab + 1) * CELLS] = lax.dot_general(
            taps_by_outs,
            r_ref[slab, :CELLS, :],
            (((1,), (1,)), ((), ())),
            preferred_element_type=F32,
        )
    low, row, col = lane_masks()
    zero = jnp.zeros((16, LANES), F32)
    for group in range(2):

        def term(along_x, along_y, along_z, column):
            if column < 0 or column >= COLUMNS:
                return zero
            start = tap_index(along_x, along_y, along_z) * OUTS + group * 16
            return z_ref[start : start + 16, column * LANES : (column + 1) * LANES]

        grads = []
        for column in range(COLUMNS):
            total = None
            for c in range(3):
                over_y = None
                for b in range(3):
                    mixed = jnp.where(
                        low,
                        term(2, b, c, column + 1) + term(0, b, c, column),
                        term(2, b, c, column) + term(0, b, c, column - 1),
                    )
                    over_x = term(1, b, c, column) + turn(mixed, 64)
                    if b != 1:
                        over_x = jnp.where(inside(row, b - 1), turn(over_x, -8 * (b - 1)), 0.0)
                    over_y = over_x if over_y is None else over_y + over_x
                if c != 1:
                    over_y = jnp.where(inside(col, c - 1), turn(over_y, -(c - 1)), 0.0)
                total = over_y if total is None else total + over_y
            slab, part = column // 2, column % 2
            lanes = slice(part * LANES, (part + 1) * LANES)
            logistic = 1.0 / (1.0 + jnp.exp(-total))
            out_ref[slab, CELLS + group * 16 : CELLS + group * 16 + 16, lanes] = (
                total * logistic
            ).astype(BF16)
            upstream = r_ref[
                slab, CELLS + group * 16 : CELLS + group * 16 + 16, lanes
            ].astype(F32)
            grad = upstream * (logistic * (1.0 + total * (1.0 - logistic)))
            grads.append(grad.astype(BF16).astype(F32))
        for c in range(3):
            if c == 1:
                by_z = grads
            else:
                by_z = [jnp.where(inside(col, 1 - c), turn(g, c - 1), 0.0) for g in grads]
            for b in range(3):
                if b == 1:
                    by_y = by_z
                else:
                    by_y = [
                        jnp.where(inside(row, 1 - b), turn(g, 8 * (b - 1)), 0.0) for g in by_z
                    ]
                swapped = [zero] + [turn(g, 64) for g in by_y] + [zero]
                for column in range(COLUMNS):
                    lanes = slice(column * LANES, (column + 1) * LANES)
                    here = swapped[column + 1]
                    for a, value in (
                        (0, jnp.where(low, here, swapped[column + 2])),
                        (1, by_y[column]),
                        (2, jnp.where(low, swapped[column], here)),
                    ):
                        start = tap_index(a, b, c) * OUTS + group * 16
                        g_ref[start : start + 16, lanes] = value.astype(BF16)
    whole = jnp.dot(
        g_ref[: TAPS * OUTS, :],
        r_ref[:, :CELLS, :].reshape(WHOLE, CELLS),
        preferred_element_type=F32,
    )
    for tap in range(TAPS):
        start = tap * OUTS
        left = whole[start : start + 16]
        right = whole[start + 16 : start + 32]
        own_ref[tap * 16 : tap * 16 + 16, :] = jnp.where(first, left, right)
        other_ref[tap * 16 : tap * 16 + 16, :] = jnp.where(first, right, left).astype(
            other_ref.dtype
        )
    turned = jnp.transpose(w2_ref[...].astype(F32)).astype(BF16)
    for slab in range(SLABS):
        out_ref[slab, :CELLS, :] = jnp.dot(
            turned, g_ref[:, slab * CELLS : (slab + 1) * CELLS], preferred_element_type=F32
        ).astype(BF16)


def lengthen_kernel(rows_ref, after_ref, out_ref):
    out_ref[: TAPS * 16, :] = rows_ref[...]
    out_ref[TAPS * 16 :, :] = jnp.zeros((out_ref.shape[0] - TAPS * 16, CELLS), BF16)


def share_kernel(parts_ref, out_ref):
    total = parts_ref[0].astype(F32)
    for place in range(1, parts_ref.shape[0]):
        total = total + parts_ref[place].astype(F32)
    for place in range(out_ref.shape[0]):
        out_ref[place] = total.astype(BF16)


def final_kernel(chip_ref, r_ref, act_ref, grad_ref):
    total = r_ref[0, :CELLS, :].astype(F32)
    for slab in range(1, SLABS):
        total = total + r_ref[slab, :CELLS, :].astype(F32)
    grad_ref[...] = jnp.transpose(total).astype(BF16)
    for half in range(2):
        turned = jnp.transpose(
            jnp.concatenate(
                [
                    r_ref[(pair + chip_ref[0]) & 7, CELLS:, :].astype(F32)
                    for pair in range(half * 4, half * 4 + 4)
                ],
                axis=0,
            )
        )
        act_ref[:, half * LANES : (half + 1) * LANES] = turned.astype(BF16)


VMEM = pl.BlockSpec(memory_space=pltpu.VMEM)
SMEM = pl.BlockSpec(memory_space=pltpu.SMEM)
PARAMS = pltpu.CompilerParams(vmem_limit_bytes=48 * 1024 * 1024)


def shape(*dims, dtype=BF16):
    return jax.ShapeDtypeStruct(dims, dtype)


def call(kernel, outs, operands, specs=None, scratch=(), flops=0):
    moved = sum(a.size * a.dtype.itemsize for a in list(operands) + list(outs))
    return pl.pallas_call(
        kernel,
        out_shape=tuple(outs),
        in_specs=specs or [VMEM] * len(operands),
        out_specs=tuple(VMEM for _ in outs),
        scratch_shapes=list(scratch),
        compiler_params=PARAMS,
        cost_estimate=pl.CostEstimate(flops=flops, bytes_accessed=moved, transcendentals=0),
    )(*operands)


def local(inputs, weights, upstream):
    owner = lax.axis_index("fsdp")
    core = (owner % 2).astype(jnp.int32).reshape(1)
    chip = (owner // 2).astype(jnp.int32).reshape(1)
    chips = lax.axis_size("fsdp") // 2
    reps = lax.axis_size("rep")
    total_cells = 2 * chips * reps * WHOLE
    factor = float(total_cells) ** (-0.5)

    def place(z, core, y, rep):
        return ((z * 2 + core) * SLABS + y) * reps + rep

    everyone = ("fsdp", "slab", "rep")
    mirrored = [
        (place(z, core, y, rep), place((y - z) % SLABS, core, y, rep))
        for z in range(chips)
        for core in range(2)
        for y in range(SLABS)
        for rep in range(reps)
    ]
    cores = [(2 * z + core, 2 * z + 1 - core) for z in range(chips) for core in range(2)]

    by_tap = jnp.transpose(weights, (1, 0, 2))
    same = lax.ppermute(by_tap, everyone, mirrored)
    opposite = lax.ppermute(same, "fsdp", cores)

    cells = inputs.reshape(CELLS, CELLS)
    packed = call(
        pack_kernel,
        [shape(SLABS, CELLS + OUTS, CELLS)],
        (chip, cells, upstream.reshape(CELLS, CELLS)),
        specs=[SMEM, VMEM, VMEM],
    )[0]
    gathered = lax.all_to_all(packed, "slab", 0, 0)

    terms, own, other = call(
        main_kernel,
        [
            shape(SLABS, CELLS + OUTS, CELLS),
            shape(TAPS * 16, CELLS, dtype=F32),
            shape(TAPS * 16, CELLS, dtype=F32),
        ],
        (core, gathered, same, opposite),
        specs=[SMEM, VMEM, VMEM, VMEM],
        scratch=[
            pltpu.VMEM((ROWS, WHOLE), BF16),
            pltpu.VMEM((ROWS, CELLS), BF16),
            pltpu.VMEM((TAPS * OUTS, WHOLE), F32),
        ],
        flops=6 * ROWS * WHOLE * CELLS,
    )
    returned = lax.all_to_all(terms, "slab", 0, 0)
    activated, input_grad = call(
        final_kernel,
        [shape(CELLS, CELLS), shape(CELLS, CELLS)],
        (chip, returned),
        specs=[SMEM, VMEM],
    )

    sums = (own + lax.ppermute(other, "fsdp", cores)).astype(BF16)
    sums = lax.ppermute(sums, everyone, mirrored)
    plane = SLABS * reps
    sums = call(
        lengthen_kernel,
        [shape(512, CELLS)],
        (sums, returned),
        specs=[VMEM, pl.BlockSpec(memory_space=pl.ANY)],
    )[0]
    scattered = lax.all_to_all(
        sums.reshape(plane, 512 // plane, CELLS), ("slab", "rep"), 0, 0
    )
    share = call(share_kernel, [shape(plane, 512 // plane, CELLS)], (scattered,))[0]
    parts = lax.all_to_all(share, ("slab", "rep"), 0, 0).astype(F32)
    weight_grad = jnp.transpose(parts.reshape(32, 16, CELLS)[:TAPS], (1, 0, 2)) * factor
    return (
        activated.reshape(inputs.shape),
        input_grad.reshape(inputs.shape),
        weight_grad,
    )


def solution(mesh):
    placed = (
        P(("fsdp", "rep"), "slab", None, None, None),
        P("fsdp", None, None),
        P(("fsdp", "rep"), "slab", None, None, None),
    )
    return jax.shard_map(
        local,
        mesh=mesh,
        in_specs=placed,
        out_specs=(
            P(("fsdp", "rep"), "slab", None, None, None),
            P(("fsdp", "rep"), "slab", None, None, None),
            P("fsdp", None, None),
        ),
        check_vma=False,
    )
```

```python
import jax
import jax.numpy as jnp
from jax import lax
from jax.experimental import pallas as pl
from jax.experimental.pallas import tpu as pltpu
from jax.sharding import PartitionSpec as P

F32 = jnp.float32
BF16 = jnp.bfloat16
CELLS = 256
LANES = 128
SLABS = 8
OUTS = 32
TAPS = 27
ROWS = 28 * OUTS
WHOLE = SLABS * CELLS
COLUMNS = WHOLE // LANES


def tap_index(along_x, along_y, along_z):
    return (along_x * 3 + along_y) * 3 + along_z


def home(pair, core, chip):
    return (pair + 4 * core + chip) & 7


def pack_kernel(chip_ref, x_ref, u_ref, out_ref, x_own, u_own, turned, sems):
    take_u = pltpu.make_async_copy(u_ref, u_own, sems.at[0])
    take_x = pltpu.make_async_copy(x_ref, x_own, sems.at[1])
    take_u.start()
    take_x.start()
    take_x.wait()
    copies = [
        pltpu.make_async_copy(x_own, out_ref.at[slab, pl.ds(0, CELLS), :], sems.at[2 + slab])
        for slab in range(SLABS)
    ]
    for copy in copies:
        copy.start()
    take_u.wait()
    by_out = jnp.transpose(u_own[...].astype(F32)).astype(BF16)
    for pair in range(SLABS):
        for core in range(2):
            start = pair * OUTS + core * 16
            turned[home(pair, core, chip_ref[0]), core * 16 : core * 16 + 16, :] = by_out[
                start : start + 16
            ]
    last = pltpu.make_async_copy(
        turned, out_ref.at[:, pl.ds(CELLS, OUTS), :], sems.at[2 + SLABS]
    )
    last.start()
    for copy in copies:
        copy.wait()
    last.wait()


def lane_masks():
    lane = lax.broadcasted_iota(jnp.int32, (16, LANES), 1)
    row = (lane >> 3) & 7
    col = lane & 7
    return lane < 64, row, col


def inside(coordinate, shift):
    moved = coordinate + shift
    return (moved >= 0) & (moved < 8)


def turn(block, shift):
    return pltpu.roll(block, shift % LANES, 1)


def main_kernel(
    core_ref, r_ref, same_ref, opposite_ref, out_ref, own_ref, other_ref, g_ref, w2_ref, z_ref
):
    first = core_ref[0] == 0
    for tap in range(TAPS):
        start = tap * OUTS
        same, opposite = same_ref[tap], opposite_ref[tap]
        w2_ref[start : start + 16, :] = jnp.where(first, same, opposite)
        w2_ref[start + 16 : start + 32, :] = jnp.where(first, opposite, same)
    w2_ref[TAPS * OUTS :, :] = jnp.zeros((OUTS, CELLS), BF16)
    g_ref[TAPS * OUTS :, :] = jnp.zeros((OUTS, WHOLE), BF16)
    taps_by_outs = w2_ref[: TAPS * OUTS, :]
    for slab in range(SLABS):
        z_ref[:, slab * CELLS : (slab + 1) * CELLS] = lax.dot_general(
            taps_by_outs,
            r_ref[slab, :CELLS, :],
            (((1,), (1,)), ((), ())),
            preferred_element_type=F32,
        )
    low, row, col = lane_masks()
    zero = jnp.zeros((16, LANES), F32)
    for group in range(2):

        def term(along_x, along_y, along_z, column):
            if column < 0 or column >= COLUMNS:
                return zero
            start = tap_index(along_x, along_y, along_z) * OUTS + group * 16
            return z_ref[start : start + 16, column * LANES : (column + 1) * LANES]

        grads = []
        for column in range(COLUMNS):
            total = None
            for c in range(3):
                over_y = None
                for b in range(3):
                    mixed = jnp.where(
                        low,
                        term(2, b, c, column + 1) + term(0, b, c, column),
                        term(2, b, c, column) + term(0, b, c, column - 1),
                    )
                    over_x = term(1, b, c, column) + turn(mixed, 64)
                    if b != 1:
                        over_x = jnp.where(inside(row, b - 1), turn(over_x, -8 * (b - 1)), 0.0)
                    over_y = over_x if over_y is None else over_y + over_x
                if c != 1:
                    over_y = jnp.where(inside(col, c - 1), turn(over_y, -(c - 1)), 0.0)
                total = over_y if total is None else total + over_y
            slab, part = column // 2, column % 2
            lanes = slice(part * LANES, (part + 1) * LANES)
            logistic = 1.0 / (1.0 + jnp.exp(-total))
            out_ref[slab, CELLS + group * 16 : CELLS + group * 16 + 16, lanes] = (
                total * logistic
            ).astype(BF16)
            upstream = r_ref[
                slab, CELLS + group * 16 : CELLS + group * 16 + 16, lanes
            ].astype(F32)
            grad = upstream * (logistic * (1.0 + total * (1.0 - logistic)))
            grads.append(grad.astype(BF16).astype(F32))
        for c in range(3):
            if c == 1:
                by_z = grads
            else:
                by_z = [jnp.where(inside(col, 1 - c), turn(g, c - 1), 0.0) for g in grads]
            for b in range(3):
                if b == 1:
                    by_y = by_z
                else:
                    by_y = [
                        jnp.where(inside(row, 1 - b), turn(g, 8 * (b - 1)), 0.0) for g in by_z
                    ]
                swapped = [zero] + [turn(g, 64) for g in by_y] + [zero]
                for column in range(COLUMNS):
                    lanes = slice(column * LANES, (column + 1) * LANES)
                    here = swapped[column + 1]
                    for a, value in (
                        (0, jnp.where(low, here, swapped[column + 2])),
                        (1, by_y[column]),
                        (2, jnp.where(low, swapped[column], here)),
                    ):
                        start = tap_index(a, b, c) * OUTS + group * 16
                        g_ref[start : start + 16, lanes] = value.astype(BF16)
    whole = jnp.dot(
        g_ref[: TAPS * OUTS, :],
        r_ref[:, :CELLS, :].reshape(WHOLE, CELLS),
        preferred_element_type=F32,
    )
    for tap in range(TAPS):
        start = tap * OUTS
        left = whole[start : start + 16]
        right = whole[start + 16 : start + 32]
        own_ref[tap * 16 : tap * 16 + 16, :] = jnp.where(first, left, right)
        other_ref[tap * 16 : tap * 16 + 16, :] = jnp.where(first, right, left).astype(
            other_ref.dtype
        )
    turned = jnp.transpose(w2_ref[...].astype(F32)).astype(BF16)
    for slab in range(SLABS):
        out_ref[slab, :CELLS, :] = jnp.dot(
            turned, g_ref[:, slab * CELLS : (slab + 1) * CELLS], preferred_element_type=F32
        ).astype(BF16)


def lengthen_kernel(rows_ref, after_ref, out_ref):
    out_ref[: TAPS * 16, :] = rows_ref[...]
    out_ref[TAPS * 16 :, :] = jnp.zeros((out_ref.shape[0] - TAPS * 16, CELLS), BF16)


def share_kernel(parts_ref, out_ref):
    total = parts_ref[0].astype(F32)
    for place in range(1, parts_ref.shape[0]):
        total = total + parts_ref[place].astype(F32)
    for place in range(out_ref.shape[0]):
        out_ref[place] = total.astype(BF16)


def final_kernel(chip_ref, r_ref, act_ref, grad_ref):
    total = r_ref[0, :CELLS, :].astype(F32)
    for slab in range(1, SLABS):
        total = total + r_ref[slab, :CELLS, :].astype(F32)
    grad_ref[...] = jnp.transpose(total).astype(BF16)
    for half in range(2):
        turned = jnp.transpose(
            jnp.concatenate(
                [
                    r_ref[
                        home(pair, core, chip_ref[0]),
                        CELLS + core * 16 : CELLS + core * 16 + 16,
                        :,
                    ].astype(F32)
                    for pair in range(half * 4, half * 4 + 4)
                    for core in range(2)
                ],
                axis=0,
            )
        )
        act_ref[:, half * LANES : (half + 1) * LANES] = turned.astype(BF16)


VMEM = pl.BlockSpec(memory_space=pltpu.VMEM)
SMEM = pl.BlockSpec(memory_space=pltpu.SMEM)
ANY = pl.BlockSpec(memory_space=pl.ANY)
HBM = pl.BlockSpec(memory_space=pltpu.HBM)


def shape(*dims, dtype=BF16):
    return jax.ShapeDtypeStruct(dims, dtype)


def call(kernel, outs, operands, specs=None, scratch=(), flops=0, out_spec=VMEM, vmem=48):
    moved = sum(a.size * a.dtype.itemsize for a in list(operands) + list(outs))
    return pl.pallas_call(
        kernel,
        out_shape=tuple(outs),
        in_specs=specs or [VMEM] * len(operands),
        out_specs=tuple(out_spec for _ in outs),
        scratch_shapes=list(scratch),
        compiler_params=pltpu.CompilerParams(vmem_limit_bytes=vmem * 1024 * 1024),
        cost_estimate=pl.CostEstimate(flops=flops, bytes_accessed=moved, transcendentals=0),
    )(*operands)


def local(inputs, weights, upstream):
    owner = lax.axis_index("fsdp")
    core = (owner % 2).astype(jnp.int32).reshape(1)
    chip = (owner // 2).astype(jnp.int32).reshape(1)
    chips = lax.axis_size("fsdp") // 2
    reps = lax.axis_size("rep")
    total_cells = 2 * chips * reps * WHOLE
    factor = float(total_cells) ** (-0.5)

    def place(z, core, y, rep):
        return ((z * 2 + core) * SLABS + y) * reps + rep

    everyone = ("fsdp", "slab", "rep")
    mirrored = [
        (place(z, core, y, rep), place((y + 4 * core - z) % SLABS, core, y, rep))
        for z in range(chips)
        for core in range(2)
        for y in range(SLABS)
        for rep in range(reps)
    ]
    cores = [(2 * z + core, 2 * z + 1 - core) for z in range(chips) for core in range(2)]

    by_tap = jnp.transpose(weights, (1, 0, 2))
    same = lax.ppermute(by_tap, everyone, mirrored)
    opposite = lax.ppermute(same, "fsdp", cores)

    cells = inputs.reshape(CELLS, CELLS)
    packed = call(
        pack_kernel,
        [shape(SLABS, CELLS + OUTS, CELLS)],
        (chip, cells, upstream.reshape(CELLS, CELLS)),
        specs=[SMEM, HBM, HBM],
        scratch=[
            pltpu.VMEM((CELLS, CELLS), BF16),
            pltpu.VMEM((CELLS, CELLS), BF16),
            pltpu.VMEM((SLABS, OUTS, CELLS), BF16),
            pltpu.SemaphoreType.DMA((3 + SLABS,)),
        ],
        out_spec=HBM,
        vmem=56,
    )[0]
    gathered = lax.all_to_all(packed, "slab", 0, 0)

    terms, own, other = call(
        main_kernel,
        [
            shape(SLABS, CELLS + OUTS, CELLS),
            shape(TAPS * 16, CELLS, dtype=F32),
            shape(TAPS * 16, CELLS, dtype=F32),
        ],
        (core, gathered, same, opposite),
        specs=[SMEM, VMEM, VMEM, VMEM],
        scratch=[
            pltpu.VMEM((ROWS, WHOLE), BF16),
            pltpu.VMEM((ROWS, CELLS), BF16),
            pltpu.VMEM((TAPS * OUTS, WHOLE), F32),
        ],
        flops=6 * ROWS * WHOLE * CELLS,
    )
    returned = lax.all_to_all(terms, "slab", 0, 0)
    activated, input_grad = call(
        final_kernel,
        [shape(CELLS, CELLS), shape(CELLS, CELLS)],
        (chip, returned),
        specs=[SMEM, VMEM],
    )

    sums = (own + lax.ppermute(other, "fsdp", cores)).astype(BF16)
    sums = lax.ppermute(sums, everyone, mirrored)
    plane = SLABS * reps
    sums = call(
        lengthen_kernel,
        [shape(512, CELLS)],
        (sums, returned),
        specs=[VMEM, ANY],
    )[0]
    scattered = lax.all_to_all(
        sums.reshape(plane, 512 // plane, CELLS), ("slab", "rep"), 0, 0
    )
    share = call(share_kernel, [shape(plane, 512 // plane, CELLS)], (scattered,))[0]
    parts = lax.all_to_all(share, ("slab", "rep"), 0, 0).astype(F32)
    weight_grad = jnp.transpose(parts.reshape(32, 16, CELLS)[:TAPS], (1, 0, 2)) * factor
    return (
        activated.reshape(inputs.shape),
        input_grad.reshape(inputs.shape),
        weight_grad,
    )


def solution(mesh):
    placed = (
        P(("fsdp", "rep"), "slab", None, None, None),
        P("fsdp", None, None),
        P(("fsdp", "rep"), "slab", None, None, None),
    )
    return jax.shard_map(
        local,
        mesh=mesh,
        in_specs=placed,
        out_specs=(
            P(("fsdp", "rep"), "slab", None, None, None),
            P(("fsdp", "rep"), "slab", None, None, None),
            P("fsdp", None, None),
        ),
        check_vma=False,
    )
```

```python
import jax
import jax.numpy as jnp
from jax import lax
from jax.experimental import pallas as pl
from jax.experimental.pallas import tpu as pltpu
from jax.sharding import PartitionSpec as P

F32 = jnp.float32
BF16 = jnp.bfloat16
CELLS = 256
LANES = 128
SLABS = 8
OUTS = 32
TAPS = 27
ROWS = 28 * OUTS
WHOLE = SLABS * CELLS
COLUMNS = WHOLE // LANES
AHEAD = 2 * 10**10


def tap_index(along_x, along_y, along_z):
    return (along_x * 3 + along_y) * 3 + along_z


def home(pair, core, chip):
    return (pair + 4 * core + chip) & 7


def pack_kernel(chip_ref, x_ref, u_ref, out_ref, x_own, u_own, turned, sems):
    take_u = pltpu.make_async_copy(u_ref, u_own, sems.at[0])
    take_x = pltpu.make_async_copy(x_ref, x_own, sems.at[1])
    take_u.start()
    take_x.start()
    take_x.wait()
    copies = [
        pltpu.make_async_copy(x_own, out_ref.at[slab, pl.ds(0, CELLS), :], sems.at[2 + slab])
        for slab in range(SLABS)
    ]
    for copy in copies:
        copy.start()
    take_u.wait()
    by_out = jnp.transpose(u_own[...].astype(F32)).astype(BF16)
    for pair in range(SLABS):
        for core in range(2):
            start = pair * OUTS + core * 16
            turned[home(pair, core, chip_ref[0]), core * 16 : core * 16 + 16, :] = by_out[
                start : start + 16
            ]
    last = pltpu.make_async_copy(
        turned, out_ref.at[:, pl.ds(CELLS, OUTS), :], sems.at[2 + SLABS]
    )
    last.start()
    for copy in copies:
        copy.wait()
    last.wait()


def lane_masks():
    lane = lax.broadcasted_iota(jnp.int32, (16, LANES), 1)
    row = (lane >> 3) & 7
    col = lane & 7
    return lane < 64, row, col


def inside(coordinate, shift):
    moved = coordinate + shift
    return (moved >= 0) & (moved < 8)


def turn(block, shift):
    return pltpu.roll(block, shift % LANES, 1)


def main_kernel(
    core_ref, r_ref, same_ref, opposite_ref, out_ref, own_ref, other_ref, g_ref, w2_ref, z_ref
):
    first = core_ref[0] == 0
    for tap in range(TAPS):
        start = tap * OUTS
        same, opposite = same_ref[tap], opposite_ref[tap]
        w2_ref[start : start + 16, :] = jnp.where(first, same, opposite)
        w2_ref[start + 16 : start + 32, :] = jnp.where(first, opposite, same)
    w2_ref[TAPS * OUTS :, :] = jnp.zeros((OUTS, CELLS), BF16)
    g_ref[TAPS * OUTS :, :] = jnp.zeros((OUTS, WHOLE), BF16)
    taps_by_outs = w2_ref[: TAPS * OUTS, :]
    for slab in range(SLABS):
        z_ref[:, slab * CELLS : (slab + 1) * CELLS] = lax.dot_general(
            taps_by_outs,
            r_ref[slab, :CELLS, :],
            (((1,), (1,)), ((), ())),
            preferred_element_type=F32,
        )
    low, row, col = lane_masks()
    zero = jnp.zeros((16, LANES), F32)
    for group in range(2):

        def term(along_x, along_y, along_z, column):
            if column < 0 or column >= COLUMNS:
                return zero
            start = tap_index(along_x, along_y, along_z) * OUTS + group * 16
            return z_ref[start : start + 16, column * LANES : (column + 1) * LANES]

        grads = []
        for column in range(COLUMNS):
            total = None
            for c in range(3):
                over_y = None
                for b in range(3):
                    mixed = jnp.where(
                        low,
                        term(2, b, c, column + 1) + term(0, b, c, column),
                        term(2, b, c, column) + term(0, b, c, column - 1),
                    )
                    over_x = term(1, b, c, column) + turn(mixed, 64)
                    if b != 1:
                        over_x = jnp.where(inside(row, b - 1), turn(over_x, -8 * (b - 1)), 0.0)
                    over_y = over_x if over_y is None else over_y + over_x
                if c != 1:
                    over_y = jnp.where(inside(col, c - 1), turn(over_y, -(c - 1)), 0.0)
                total = over_y if total is None else total + over_y
            slab, part = column // 2, column % 2
            lanes = slice(part * LANES, (part + 1) * LANES)
            logistic = 1.0 / (1.0 + jnp.exp(-total))
            out_ref[slab, CELLS + group * 16 : CELLS + group * 16 + 16, lanes] = (
                total * logistic
            ).astype(BF16)
            upstream = r_ref[
                slab, CELLS + group * 16 : CELLS + group * 16 + 16, lanes
            ].astype(F32)
            grad = upstream * (logistic * (1.0 + total * (1.0 - logistic)))
            grads.append(grad.astype(BF16).astype(F32))
        for c in range(3):
            if c == 1:
                by_z = grads
            else:
                by_z = [jnp.where(inside(col, 1 - c), turn(g, c - 1), 0.0) for g in grads]
            for b in range(3):
                if b == 1:
                    by_y = by_z
                else:
                    by_y = [
                        jnp.where(inside(row, 1 - b), turn(g, 8 * (b - 1)), 0.0) for g in by_z
                    ]
                swapped = [zero] + [turn(g, 64) for g in by_y] + [zero]
                for column in range(COLUMNS):
                    lanes = slice(column * LANES, (column + 1) * LANES)
                    here = swapped[column + 1]
                    for a, value in (
                        (0, jnp.where(low, here, swapped[column + 2])),
                        (1, by_y[column]),
                        (2, jnp.where(low, swapped[column], here)),
                    ):
                        start = tap_index(a, b, c) * OUTS + group * 16
                        g_ref[start : start + 16, lanes] = value.astype(BF16)
    whole = jnp.dot(
        g_ref[: TAPS * OUTS, :],
        r_ref[:, :CELLS, :].reshape(WHOLE, CELLS),
        preferred_element_type=F32,
    )
    for tap in range(TAPS):
        start = tap * OUTS
        left = whole[start : start + 16]
        right = whole[start + 16 : start + 32]
        own_ref[tap * 16 : tap * 16 + 16, :] = jnp.where(first, left, right)
        other_ref[tap * 16 : tap * 16 + 16, :] = jnp.where(first, right, left).astype(
            other_ref.dtype
        )
    turned = jnp.transpose(w2_ref[...].astype(F32)).astype(BF16)
    for slab in range(SLABS):
        out_ref[slab, :CELLS, :] = jnp.dot(
            turned, g_ref[:, slab * CELLS : (slab + 1) * CELLS], preferred_element_type=F32
        ).astype(BF16)


def copy_kernel(rows_ref, out_ref):
    out_ref[...] = rows_ref[...]


def add_kernel(own_ref, got_ref, out_ref):
    out_ref[...] = (own_ref[...] + got_ref[...]).astype(BF16)


def lengthen_kernel(rows_ref, after_ref, out_ref):
    out_ref[: TAPS * 16, :] = rows_ref[...]
    out_ref[TAPS * 16 :, :] = jnp.zeros((out_ref.shape[0] - TAPS * 16, CELLS), BF16)


def share_kernel(parts_ref, out_ref):
    total = parts_ref[0].astype(F32)
    for place in range(1, parts_ref.shape[0]):
        total = total + parts_ref[place].astype(F32)
    for place in range(out_ref.shape[0]):
        out_ref[place] = total.astype(BF16)


def final_kernel(chip_ref, r_ref, act_ref, grad_ref):
    total = r_ref[0, :CELLS, :].astype(F32)
    for slab in range(1, SLABS):
        total = total + r_ref[slab, :CELLS, :].astype(F32)
    grad_ref[...] = jnp.transpose(total).astype(BF16)
    for half in range(2):
        turned = jnp.transpose(
            jnp.concatenate(
                [
                    r_ref[
                        home(pair, core, chip_ref[0]),
                        CELLS + core * 16 : CELLS + core * 16 + 16,
                        :,
                    ].astype(F32)
                    for pair in range(half * 4, half * 4 + 4)
                    for core in range(2)
                ],
                axis=0,
            )
        )
        act_ref[:, half * LANES : (half + 1) * LANES] = turned.astype(BF16)


VMEM = pl.BlockSpec(memory_space=pltpu.VMEM)
SMEM = pl.BlockSpec(memory_space=pltpu.SMEM)
ANY = pl.BlockSpec(memory_space=pl.ANY)
HBM = pl.BlockSpec(memory_space=pltpu.HBM)


def shape(*dims, dtype=BF16):
    return jax.ShapeDtypeStruct(dims, dtype)


def call(kernel, outs, operands, specs=None, scratch=(), flops=0, out_spec=VMEM, vmem=48):
    moved = sum(a.size * a.dtype.itemsize for a in list(operands) + list(outs))
    return pl.pallas_call(
        kernel,
        out_shape=tuple(outs),
        in_specs=specs or [VMEM] * len(operands),
        out_specs=tuple(out_spec for _ in outs),
        scratch_shapes=list(scratch),
        compiler_params=pltpu.CompilerParams(vmem_limit_bytes=vmem * 1024 * 1024),
        cost_estimate=pl.CostEstimate(flops=flops, bytes_accessed=moved, transcendentals=0),
    )(*operands)


def local(inputs, weights, upstream):
    owner = lax.axis_index("fsdp")
    core = (owner % 2).astype(jnp.int32).reshape(1)
    chip = (owner // 2).astype(jnp.int32).reshape(1)
    chips = lax.axis_size("fsdp") // 2
    reps = lax.axis_size("rep")
    total_cells = 2 * chips * reps * WHOLE
    factor = float(total_cells) ** (-0.5)

    def place(z, core, y, rep):
        return ((z * 2 + core) * SLABS + y) * reps + rep

    everyone = ("fsdp", "slab", "rep")
    mirrored = [
        (place(z, core, y, rep), place((y + 4 * core - z) % SLABS, core, y, rep))
        for z in range(chips)
        for core in range(2)
        for y in range(SLABS)
        for rep in range(reps)
    ]
    cores = [(2 * z + core, 2 * z + 1 - core) for z in range(chips) for core in range(2)]

    by_tap = jnp.transpose(weights, (1, 0, 2))
    same = lax.ppermute(by_tap, everyone, mirrored)
    onward = call(copy_kernel, [shape(TAPS, 16, CELLS)], (same,), flops=AHEAD)[0]
    opposite = lax.ppermute(onward, "fsdp", cores)

    cells = inputs.reshape(CELLS, CELLS)
    packed = call(
        pack_kernel,
        [shape(SLABS, CELLS + OUTS, CELLS)],
        (chip, cells, upstream.reshape(CELLS, CELLS)),
        specs=[SMEM, HBM, HBM],
        scratch=[
            pltpu.VMEM((CELLS, CELLS), BF16),
            pltpu.VMEM((CELLS, CELLS), BF16),
            pltpu.VMEM((SLABS, OUTS, CELLS), BF16),
            pltpu.SemaphoreType.DMA((3 + SLABS,)),
        ],
        out_spec=HBM,
        vmem=56,
    )[0]
    gathered = lax.all_to_all(packed, "slab", 0, 0)

    terms, own, other = call(
        main_kernel,
        [
            shape(SLABS, CELLS + OUTS, CELLS),
            shape(TAPS * 16, CELLS, dtype=F32),
            shape(TAPS * 16, CELLS, dtype=F32),
        ],
        (core, gathered, same, opposite),
        specs=[SMEM, VMEM, VMEM, VMEM],
        scratch=[
            pltpu.VMEM((ROWS, WHOLE), BF16),
            pltpu.VMEM((ROWS, CELLS), BF16),
            pltpu.VMEM((TAPS * OUTS, WHOLE), F32),
        ],
        flops=6 * ROWS * WHOLE * CELLS,
    )
    returned = lax.all_to_all(terms, "slab", 0, 0)
    activated, input_grad = call(
        final_kernel,
        [shape(CELLS, CELLS), shape(CELLS, CELLS)],
        (chip, returned),
        specs=[SMEM, VMEM],
    )

    sums = call(
        add_kernel,
        [shape(TAPS * 16, CELLS)],
        (own, lax.ppermute(other, "fsdp", cores)),
        flops=AHEAD,
    )[0]
    sums = lax.ppermute(sums, everyone, mirrored)
    plane = SLABS * reps
    sums = call(
        lengthen_kernel,
        [shape(512, CELLS)],
        (sums, returned),
        specs=[VMEM, ANY],
    )[0]
    scattered = lax.all_to_all(
        sums.reshape(plane, 512 // plane, CELLS), ("slab", "rep"), 0, 0
    )
    share = call(share_kernel, [shape(plane, 512 // plane, CELLS)], (scattered,))[0]
    parts = lax.all_to_all(share, ("slab", "rep"), 0, 0).astype(F32)
    weight_grad = jnp.transpose(parts.reshape(32, 16, CELLS)[:TAPS], (1, 0, 2)) * factor
    return (
        activated.reshape(inputs.shape),
        input_grad.reshape(inputs.shape),
        weight_grad,
    )


def solution(mesh):
    placed = (
        P(("fsdp", "rep"), "slab", None, None, None),
        P("fsdp", None, None),
        P(("fsdp", "rep"), "slab", None, None, None),
    )
    return jax.shard_map(
        local,
        mesh=mesh,
        in_specs=placed,
        out_specs=(
            P(("fsdp", "rep"), "slab", None, None, None),
            P(("fsdp", "rep"), "slab", None, None, None),
            P("fsdp", None, None),
        ),
        check_vma=False,
    )
```

```python
import functools

import jax
import jax.numpy as jnp
from jax import lax
from jax.experimental import pallas as pl
from jax.experimental.pallas import tpu as pltpu
from jax.sharding import PartitionSpec as P

F32 = jnp.float32
BF16 = jnp.bfloat16
CELLS = 256
LANES = 128
SLABS = 8
OUTS = 32
TAPS = 27
HALF = 14 * 16
ROWS = 28 * OUTS
WHOLE = SLABS * CELLS
COLUMNS = WHOLE // LANES


def tap_index(along_x, along_y, along_z):
    return (along_x * 3 + along_y) * 3 + along_z


def home(pair, core, chip):
    return (pair + 4 * core + chip) & 7


def pack_kernel(chip_ref, x_ref, u_ref, out_ref, x_own, u_own, turned, sems):
    take_u = pltpu.make_async_copy(u_ref, u_own, sems.at[0])
    take_x = pltpu.make_async_copy(x_ref, x_own, sems.at[1])
    take_u.start()
    take_x.start()
    take_x.wait()
    copies = [
        pltpu.make_async_copy(x_own, out_ref.at[slab, pl.ds(0, CELLS), :], sems.at[2 + slab])
        for slab in range(SLABS)
    ]
    for copy in copies:
        copy.start()
    take_u.wait()
    by_out = jnp.transpose(u_own[...].astype(F32)).astype(BF16)
    for pair in range(SLABS):
        for core in range(2):
            start = pair * OUTS + core * 16
            turned[home(pair, core, chip_ref[0]), core * 16 : core * 16 + 16, :] = by_out[
                start : start + 16
            ]
    last = pltpu.make_async_copy(
        turned, out_ref.at[:, pl.ds(CELLS, OUTS), :], sems.at[2 + SLABS]
    )
    last.start()
    for copy in copies:
        copy.wait()
    last.wait()


def lane_masks():
    lane = lax.broadcasted_iota(jnp.int32, (16, LANES), 1)
    row = (lane >> 3) & 7
    col = lane & 7
    return lane < 64, row, col


def inside(coordinate, shift):
    moved = coordinate + shift
    return (moved >= 0) & (moved < 8)


def turn(block, shift):
    return pltpu.roll(block, shift % LANES, 1)


def main_kernel(
    core_ref, r_ref, same_ref, opposite_ref, out_ref, own_ref, other_ref, g_ref, w2_ref, z_ref
):
    first = core_ref[0] == 0
    for tap in range(TAPS):
        start = tap * OUTS
        same, opposite = same_ref[tap], opposite_ref[tap]
        w2_ref[start : start + 16, :] = jnp.where(first, same, opposite)
        w2_ref[start + 16 : start + 32, :] = jnp.where(first, opposite, same)
    w2_ref[TAPS * OUTS :, :] = jnp.zeros((OUTS, CELLS), BF16)
    g_ref[TAPS * OUTS :, :] = jnp.zeros((OUTS, WHOLE), BF16)
    taps_by_outs = w2_ref[: TAPS * OUTS, :]
    for slab in range(SLABS):
        z_ref[:, slab * CELLS : (slab + 1) * CELLS] = lax.dot_general(
            taps_by_outs,
            r_ref[slab, :CELLS, :],
            (((1,), (1,)), ((), ())),
            preferred_element_type=F32,
        )
    low, row, col = lane_masks()
    zero = jnp.zeros((16, LANES), F32)
    for group in range(2):

        def term(along_x, along_y, along_z, column):
            if column < 0 or column >= COLUMNS:
                return zero
            start = tap_index(along_x, along_y, along_z) * OUTS + group * 16
            return z_ref[start : start + 16, column * LANES : (column + 1) * LANES]

        grads = []
        for column in range(COLUMNS):
            total = None
            for c in range(3):
                over_y = None
                for b in range(3):
                    mixed = jnp.where(
                        low,
                        term(2, b, c, column + 1) + term(0, b, c, column),
                        term(2, b, c, column) + term(0, b, c, column - 1),
                    )
                    over_x = term(1, b, c, column) + turn(mixed, 64)
                    if b != 1:
                        over_x = jnp.where(inside(row, b - 1), turn(over_x, -8 * (b - 1)), 0.0)
                    over_y = over_x if over_y is None else over_y + over_x
                if c != 1:
                    over_y = jnp.where(inside(col, c - 1), turn(over_y, -(c - 1)), 0.0)
                total = over_y if total is None else total + over_y
            slab, part = column // 2, column % 2
            lanes = slice(part * LANES, (part + 1) * LANES)
            logistic = 1.0 / (1.0 + jnp.exp(-total))
            out_ref[slab, CELLS + group * 16 : CELLS + group * 16 + 16, lanes] = (
                total * logistic
            ).astype(BF16)
            upstream = r_ref[
                slab, CELLS + group * 16 : CELLS + group * 16 + 16, lanes
            ].astype(F32)
            grad = upstream * (logistic * (1.0 + total * (1.0 - logistic)))
            grads.append(grad.astype(BF16).astype(F32))
        for c in range(3):
            if c == 1:
                by_z = grads
            else:
                by_z = [jnp.where(inside(col, 1 - c), turn(g, c - 1), 0.0) for g in grads]
            for b in range(3):
                if b == 1:
                    by_y = by_z
                else:
                    by_y = [
                        jnp.where(inside(row, 1 - b), turn(g, 8 * (b - 1)), 0.0) for g in by_z
                    ]
                swapped = [zero] + [turn(g, 64) for g in by_y] + [zero]
                for column in range(COLUMNS):
                    lanes = slice(column * LANES, (column + 1) * LANES)
                    here = swapped[column + 1]
                    for a, value in (
                        (0, jnp.where(low, here, swapped[column + 2])),
                        (1, by_y[column]),
                        (2, jnp.where(low, swapped[column], here)),
                    ):
                        start = tap_index(a, b, c) * OUTS + group * 16
                        g_ref[start : start + 16, lanes] = value.astype(BF16)
    whole = jnp.dot(
        g_ref[: TAPS * OUTS, :],
        r_ref[:, :CELLS, :].reshape(WHOLE, CELLS),
        preferred_element_type=F32,
    )
    own_ref[TAPS * 16 :, :] = jnp.zeros((16, CELLS), F32)
    other_ref[TAPS * 16 :, :] = jnp.zeros((16, CELLS), F32)
    for tap in range(TAPS):
        start = tap * OUTS
        left = whole[start : start + 16]
        right = whole[start + 16 : start + 32]
        own_ref[tap * 16 : tap * 16 + 16, :] = jnp.where(first, left, right)
        other_ref[tap * 16 : tap * 16 + 16, :] = jnp.where(first, right, left).astype(
            other_ref.dtype
        )
    turned = jnp.transpose(w2_ref[...].astype(F32)).astype(BF16)
    for slab in range(SLABS):
        out_ref[slab, :CELLS, :] = jnp.dot(
            turned, g_ref[:, slab * CELLS : (slab + 1) * CELLS], preferred_element_type=F32
        ).astype(BF16)


def halve_kernel(rep_ref, own_ref, got_ref, kept_ref, sent_ref):
    first = rep_ref[0] == 0
    low = own_ref[:HALF, :] + got_ref[:HALF, :]
    high = own_ref[HALF:, :] + got_ref[HALF:, :]
    kept_ref[...] = jnp.where(first, low, high)
    sent_ref[...] = jnp.where(first, high, low).astype(BF16)


def add_kernel(kept_ref, got_ref, out_ref):
    out_ref[...] = (kept_ref[...] + got_ref[...].astype(F32)).astype(BF16)


def lengthen_kernel(rows_ref, after_ref, out_ref):
    out_ref[:HALF, :] = rows_ref[...]
    out_ref[HALF:, :] = jnp.zeros((out_ref.shape[0] - HALF, CELLS), BF16)


def share_kernel(parts_ref, out_ref):
    total = parts_ref[0].astype(F32)
    for place in range(1, parts_ref.shape[0]):
        total = total + parts_ref[place].astype(F32)
    for place in range(out_ref.shape[0]):
        out_ref[place] = total.astype(BF16)


def settle_kernel(factor, parts_ref, out_ref):
    for tap in range(TAPS):
        rep, place = tap // 14, tap % 14
        rows = slice(place % 2 * 16, place % 2 * 16 + 16)
        out_ref[tap] = parts_ref[place // 2 * 2 + rep, rows, :].astype(F32) * factor


def final_kernel(chip_ref, r_ref, act_ref, grad_ref):
    total = r_ref[0, :CELLS, :].astype(F32)
    for slab in range(1, SLABS):
        total = total + r_ref[slab, :CELLS, :].astype(F32)
    grad_ref[...] = jnp.transpose(total).astype(BF16)
    for half in range(2):
        turned = jnp.transpose(
            jnp.concatenate(
                [
                    r_ref[
                        home(pair, core, chip_ref[0]),
                        CELLS + core * 16 : CELLS + core * 16 + 16,
                        :,
                    ].astype(F32)
                    for pair in range(half * 4, half * 4 + 4)
                    for core in range(2)
                ],
                axis=0,
            )
        )
        act_ref[:, half * LANES : (half + 1) * LANES] = turned.astype(BF16)


VMEM = pl.BlockSpec(memory_space=pltpu.VMEM)
SMEM = pl.BlockSpec(memory_space=pltpu.SMEM)
ANY = pl.BlockSpec(memory_space=pl.ANY)
HBM = pl.BlockSpec(memory_space=pltpu.HBM)


def shape(*dims, dtype=BF16):
    return jax.ShapeDtypeStruct(dims, dtype)


def call(kernel, outs, operands, specs=None, scratch=(), flops=0, out_spec=VMEM, vmem=48):
    moved = sum(a.size * a.dtype.itemsize for a in list(operands) + list(outs))
    return pl.pallas_call(
        kernel,
        out_shape=tuple(outs),
        in_specs=specs or [VMEM] * len(operands),
        out_specs=tuple(out_spec for _ in outs),
        scratch_shapes=list(scratch),
        compiler_params=pltpu.CompilerParams(vmem_limit_bytes=vmem * 1024 * 1024),
        cost_estimate=pl.CostEstimate(flops=flops, bytes_accessed=moved, transcendentals=0),
    )(*operands)


def local(inputs, weights, upstream):
    owner = lax.axis_index("fsdp")
    core = (owner % 2).astype(jnp.int32).reshape(1)
    chip = (owner // 2).astype(jnp.int32).reshape(1)
    rep = lax.axis_index("rep").astype(jnp.int32).reshape(1)
    chips = lax.axis_size("fsdp") // 2
    reps = lax.axis_size("rep")
    total_cells = 2 * chips * reps * WHOLE
    factor = float(total_cells) ** (-0.5)

    def place(z, core, y, rep):
        return ((z * 2 + core) * SLABS + y) * reps + rep

    everyone = ("fsdp", "slab", "rep")
    mirrored = [
        (place(z, core, y, rep), place((y + 4 * core - z) % SLABS, core, y, rep))
        for z in range(chips)
        for core in range(2)
        for y in range(SLABS)
        for rep in range(reps)
    ]
    cores = [(2 * z + core, 2 * z + 1 - core) for z in range(chips) for core in range(2)]

    by_tap = jnp.transpose(weights, (1, 0, 2))
    same = lax.ppermute(by_tap, everyone, mirrored)
    opposite = lax.ppermute(same, "fsdp", cores)

    cells = inputs.reshape(CELLS, CELLS)
    packed = call(
        pack_kernel,
        [shape(SLABS, CELLS + OUTS, CELLS)],
        (chip, cells, upstream.reshape(CELLS, CELLS)),
        specs=[SMEM, HBM, HBM],
        scratch=[
            pltpu.VMEM((CELLS, CELLS), BF16),
            pltpu.VMEM((CELLS, CELLS), BF16),
            pltpu.VMEM((SLABS, OUTS, CELLS), BF16),
            pltpu.SemaphoreType.DMA((3 + SLABS,)),
        ],
        out_spec=HBM,
        vmem=56,
    )[0]
    gathered = lax.all_to_all(packed, "slab", 0, 0)

    terms, own, other = call(
        main_kernel,
        [
            shape(SLABS, CELLS + OUTS, CELLS),
            shape(2 * HALF, CELLS, dtype=F32),
            shape(2 * HALF, CELLS, dtype=F32),
        ],
        (core, gathered, same, opposite),
        specs=[SMEM, VMEM, VMEM, VMEM],
        scratch=[
            pltpu.VMEM((ROWS, WHOLE), BF16),
            pltpu.VMEM((ROWS, CELLS), BF16),
            pltpu.VMEM((TAPS * OUTS, WHOLE), F32),
        ],
        flops=6 * ROWS * WHOLE * CELLS,
    )
    returned = lax.all_to_all(terms, "slab", 0, 0)
    activated, input_grad = call(
        final_kernel,
        [shape(CELLS, CELLS), shape(CELLS, CELLS)],
        (chip, returned),
        specs=[SMEM, VMEM],
    )

    kept, sent = call(
        halve_kernel,
        [shape(HALF, CELLS, dtype=F32), shape(HALF, CELLS)],
        (rep, own, lax.ppermute(other, "fsdp", cores)),
        specs=[SMEM, VMEM, VMEM],
    )
    got = lax.ppermute(sent, "rep", [(0, 1), (1, 0)])
    sums = call(add_kernel, [shape(HALF, CELLS)], (kept, got))[0]
    sums = lax.ppermute(sums, everyone, mirrored)
    sums = call(lengthen_kernel, [shape(256, CELLS)], (sums, returned), specs=[VMEM, ANY])[0]
    scattered = lax.all_to_all(sums.reshape(SLABS, 32, CELLS), "slab", 0, 0)
    share = call(share_kernel, [shape(SLABS * reps, 32, CELLS)], (scattered,))[0]
    parts = lax.all_to_all(share, ("slab", "rep"), 0, 0)
    weight_grad = call(
        functools.partial(settle_kernel, factor),
        [shape(TAPS, 16, CELLS, dtype=F32)],
        (parts,),
    )[0]
    weight_grad = jnp.transpose(weight_grad, (1, 0, 2))
    return (
        activated.reshape(inputs.shape),
        input_grad.reshape(inputs.shape),
        weight_grad,
    )


def solution(mesh):
    placed = (
        P(("fsdp", "rep"), "slab", None, None, None),
        P("fsdp", None, None),
        P(("fsdp", "rep"), "slab", None, None, None),
    )
    return jax.shard_map(
        local,
        mesh=mesh,
        in_specs=placed,
        out_specs=(
            P(("fsdp", "rep"), "slab", None, None, None),
            P(("fsdp", "rep"), "slab", None, None, None),
            P("fsdp", None, None),
        ),
        check_vma=False,
    )
```

```python
import jax
import jax.numpy as jnp
from jax import lax
from jax.experimental import pallas as pl
from jax.experimental.pallas import tpu as pltpu
from jax.sharding import PartitionSpec as P

F32 = jnp.float32
BF16 = jnp.bfloat16
CELLS = 256
LANES = 128
SLABS = 8
OUTS = 32
TAPS = 27
ROWS = 28 * OUTS
WHOLE = SLABS * CELLS
COLUMNS = WHOLE // LANES


def tap_index(along_x, along_y, along_z):
    return (along_x * 3 + along_y) * 3 + along_z


def home(pair, core, chip):
    return (pair + 4 * core + chip) & 7


def pack_kernel(chip_ref, x_ref, u_ref, out_ref, x_own, u_own, turned, sems):
    take_u = pltpu.make_async_copy(u_ref, u_own, sems.at[0])
    takes_x = [
        pltpu.make_async_copy(x_ref.at[rows, :], x_own.at[rows, :], sems.at[1 + part])
        for part, rows in enumerate((pl.ds(0, 128), pl.ds(128, 128)))
    ]
    for take in (takes_x[0], take_u, takes_x[1]):
        take.start()
    copies = []
    for part, rows in enumerate((pl.ds(0, 128), pl.ds(128, 128))):
        takes_x[part].wait()
        for slab in range(SLABS):
            copies.append(
                pltpu.make_async_copy(
                    x_own.at[rows, :],
                    out_ref.at[slab, rows, :],
                    sems.at[4 + part * SLABS + slab],
                )
            )
            copies[-1].start()
    take_u.wait()
    by_out = jnp.transpose(u_own[...].astype(F32)).astype(BF16)
    for pair in range(SLABS):
        for core in range(2):
            start = pair * OUTS + core * 16
            turned[home(pair, core, chip_ref[0]), core * 16 : core * 16 + 16, :] = by_out[
                start : start + 16
            ]
    last = pltpu.make_async_copy(
        turned, out_ref.at[:, pl.ds(CELLS, OUTS), :], sems.at[3]
    )
    last.start()
    for copy in copies:
        copy.wait()
    last.wait()


def lane_masks():
    lane = lax.broadcasted_iota(jnp.int32, (16, LANES), 1)
    row = (lane >> 3) & 7
    col = lane & 7
    return lane < 64, row, col


def inside(coordinate, shift):
    moved = coordinate + shift
    return (moved >= 0) & (moved < 8)


def turn(block, shift):
    return pltpu.roll(block, shift % LANES, 1)


def main_kernel(
    core_ref, r_ref, same_ref, opposite_ref, out_ref, own_ref, other_ref, g_ref, w2_ref, z_ref
):
    first = core_ref[0] == 0
    for tap in range(TAPS):
        start = tap * OUTS
        same, opposite = same_ref[tap], opposite_ref[tap]
        w2_ref[start : start + 16, :] = jnp.where(first, same, opposite)
        w2_ref[start + 16 : start + 32, :] = jnp.where(first, opposite, same)
    w2_ref[TAPS * OUTS :, :] = jnp.zeros((OUTS, CELLS), BF16)
    g_ref[TAPS * OUTS :, :] = jnp.zeros((OUTS, WHOLE), BF16)
    taps_by_outs = w2_ref[: TAPS * OUTS, :]
    for slab in range(SLABS):
        z_ref[:, slab * CELLS : (slab + 1) * CELLS] = lax.dot_general(
            taps_by_outs,
            r_ref[slab, :CELLS, :],
            (((1,), (1,)), ((), ())),
            preferred_element_type=F32,
        )
    low, row, col = lane_masks()
    zero = jnp.zeros((16, LANES), F32)
    for group in range(2):

        def term(along_x, along_y, along_z, column):
            if column < 0 or column >= COLUMNS:
                return zero
            start = tap_index(along_x, along_y, along_z) * OUTS + group * 16
            return z_ref[start : start + 16, column * LANES : (column + 1) * LANES]

        grads = []
        for column in range(COLUMNS):
            total = None
            for c in range(3):
                over_y = None
                for b in range(3):
                    mixed = jnp.where(
                        low,
                        term(2, b, c, column + 1) + term(0, b, c, column),
                        term(2, b, c, column) + term(0, b, c, column - 1),
                    )
                    over_x = term(1, b, c, column) + turn(mixed, 64)
                    if b != 1:
                        over_x = jnp.where(inside(row, b - 1), turn(over_x, -8 * (b - 1)), 0.0)
                    over_y = over_x if over_y is None else over_y + over_x
                if c != 1:
                    over_y = jnp.where(inside(col, c - 1), turn(over_y, -(c - 1)), 0.0)
                total = over_y if total is None else total + over_y
            slab, part = column // 2, column % 2
            lanes = slice(part * LANES, (part + 1) * LANES)
            logistic = 1.0 / (1.0 + jnp.exp(-total))
            out_ref[slab, CELLS + group * 16 : CELLS + group * 16 + 16, lanes] = (
                total * logistic
            ).astype(BF16)
            upstream = r_ref[
                slab, CELLS + group * 16 : CELLS + group * 16 + 16, lanes
            ].astype(F32)
            grad = upstream * (logistic * (1.0 + total * (1.0 - logistic)))
            grads.append(grad.astype(BF16).astype(F32))
        for c in range(3):
            if c == 1:
                by_z = grads
            else:
                by_z = [jnp.where(inside(col, 1 - c), turn(g, c - 1), 0.0) for g in grads]
            for b in range(3):
                if b == 1:
                    by_y = by_z
                else:
                    by_y = [
                        jnp.where(inside(row, 1 - b), turn(g, 8 * (b - 1)), 0.0) for g in by_z
                    ]
                swapped = [zero] + [turn(g, 64) for g in by_y] + [zero]
                for column in range(COLUMNS):
                    lanes = slice(column * LANES, (column + 1) * LANES)
                    here = swapped[column + 1]
                    for a, value in (
                        (0, jnp.where(low, here, swapped[column + 2])),
                        (1, by_y[column]),
                        (2, jnp.where(low, swapped[column], here)),
                    ):
                        start = tap_index(a, b, c) * OUTS + group * 16
                        g_ref[start : start + 16, lanes] = value.astype(BF16)
    whole = jnp.dot(
        g_ref[: TAPS * OUTS, :],
        r_ref[:, :CELLS, :].reshape(WHOLE, CELLS),
        preferred_element_type=F32,
    )
    for tap in range(TAPS):
        start = tap * OUTS
        left = whole[start : start + 16]
        right = whole[start + 16 : start + 32]
        own_ref[tap * 16 : tap * 16 + 16, :] = jnp.where(first, left, right)
        other_ref[tap * 16 : tap * 16 + 16, :] = jnp.where(first, right, left).astype(BF16)
    turned = jnp.transpose(w2_ref[...].astype(F32)).astype(BF16)
    for slab in range(SLABS):
        out_ref[slab, :CELLS, :] = jnp.dot(
            turned, g_ref[:, slab * CELLS : (slab + 1) * CELLS], preferred_element_type=F32
        ).astype(BF16)


def add_kernel(own_ref, got_ref, out_ref):
    out_ref[...] = (own_ref[...] + got_ref[...].astype(F32)).astype(BF16)


def lengthen_kernel(rows_ref, after_ref, out_ref):
    out_ref[: TAPS * 16, :] = rows_ref[...]
    out_ref[TAPS * 16 :, :] = jnp.zeros((out_ref.shape[0] - TAPS * 16, CELLS), BF16)


def share_kernel(parts_ref, out_ref):
    total = parts_ref[0].astype(F32)
    for place in range(1, parts_ref.shape[0]):
        total = total + parts_ref[place].astype(F32)
    for place in range(out_ref.shape[0]):
        out_ref[place] = total.astype(BF16)


def final_kernel(chip_ref, r_ref, act_ref, grad_ref):
    total = r_ref[0, :CELLS, :].astype(F32)
    for slab in range(1, SLABS):
        total = total + r_ref[slab, :CELLS, :].astype(F32)
    grad_ref[...] = jnp.transpose(total).astype(BF16)
    for half in range(2):
        turned = jnp.transpose(
            jnp.concatenate(
                [
                    r_ref[
                        home(pair, core, chip_ref[0]),
                        CELLS + core * 16 : CELLS + core * 16 + 16,
                        :,
                    ].astype(F32)
                    for pair in range(half * 4, half * 4 + 4)
                    for core in range(2)
                ],
                axis=0,
            )
        )
        act_ref[:, half * LANES : (half + 1) * LANES] = turned.astype(BF16)


VMEM = pl.BlockSpec(memory_space=pltpu.VMEM)
SMEM = pl.BlockSpec(memory_space=pltpu.SMEM)
ANY = pl.BlockSpec(memory_space=pl.ANY)
HBM = pl.BlockSpec(memory_space=pltpu.HBM)


def shape(*dims, dtype=BF16):
    return jax.ShapeDtypeStruct(dims, dtype)


def call(kernel, outs, operands, specs=None, scratch=(), flops=0, out_spec=VMEM, vmem=48):
    moved = sum(a.size * a.dtype.itemsize for a in list(operands) + list(outs))
    return pl.pallas_call(
        kernel,
        out_shape=tuple(outs),
        in_specs=specs or [VMEM] * len(operands),
        out_specs=tuple(out_spec for _ in outs),
        scratch_shapes=list(scratch),
        compiler_params=pltpu.CompilerParams(vmem_limit_bytes=vmem * 1024 * 1024),
        cost_estimate=pl.CostEstimate(flops=flops, bytes_accessed=moved, transcendentals=0),
    )(*operands)


def local(inputs, weights, upstream):
    owner = lax.axis_index("fsdp")
    core = (owner % 2).astype(jnp.int32).reshape(1)
    chip = (owner // 2).astype(jnp.int32).reshape(1)
    chips = lax.axis_size("fsdp") // 2
    reps = lax.axis_size("rep")
    total_cells = 2 * chips * reps * WHOLE
    factor = float(total_cells) ** (-0.5)

    def place(z, core, y, rep):
        return ((z * 2 + core) * SLABS + y) * reps + rep

    everyone = ("fsdp", "slab", "rep")
    mirrored = [
        (place(z, core, y, rep), place((y + 4 * core - z) % SLABS, core, y, rep))
        for z in range(chips)
        for core in range(2)
        for y in range(SLABS)
        for rep in range(reps)
    ]
    cores = [(2 * z + core, 2 * z + 1 - core) for z in range(chips) for core in range(2)]

    by_tap = jnp.transpose(weights, (1, 0, 2))
    same = lax.ppermute(by_tap, everyone, mirrored)
    opposite = lax.ppermute(same, "fsdp", cores)

    cells = inputs.reshape(CELLS, CELLS)
    packed = call(
        pack_kernel,
        [shape(SLABS, CELLS + OUTS, CELLS)],
        (chip, cells, upstream.reshape(CELLS, CELLS)),
        specs=[SMEM, HBM, HBM],
        scratch=[
            pltpu.VMEM((CELLS, CELLS), BF16),
            pltpu.VMEM((CELLS, CELLS), BF16),
            pltpu.VMEM((SLABS, OUTS, CELLS), BF16),
            pltpu.SemaphoreType.DMA((4 + 2 * SLABS,)),
        ],
        out_spec=HBM,
        vmem=56,
    )[0]
    gathered = lax.all_to_all(packed, "slab", 0, 0)

    terms, own, other = call(
        main_kernel,
        [
            shape(SLABS, CELLS + OUTS, CELLS),
            shape(TAPS * 16, CELLS, dtype=F32),
            shape(TAPS * 16, CELLS),
        ],
        (core, gathered, same, opposite),
        specs=[SMEM, VMEM, VMEM, VMEM],
        scratch=[
            pltpu.VMEM((ROWS, WHOLE), BF16),
            pltpu.VMEM((ROWS, CELLS), BF16),
            pltpu.VMEM((TAPS * OUTS, WHOLE), F32),
        ],
        flops=6 * ROWS * WHOLE * CELLS,
    )
    returned = lax.all_to_all(terms, "slab", 0, 0)
    activated, input_grad = call(
        final_kernel,
        [shape(CELLS, CELLS), shape(CELLS, CELLS)],
        (chip, returned),
        specs=[SMEM, VMEM],
    )

    sums = call(
        add_kernel, [shape(TAPS * 16, CELLS)], (own, lax.ppermute(other, "fsdp", cores))
    )[0]
    sums = lax.ppermute(sums, everyone, mirrored)
    plane = SLABS * reps
    sums = call(
        lengthen_kernel,
        [shape(512, CELLS)],
        (sums, returned),
        specs=[VMEM, ANY],
    )[0]
    scattered = lax.all_to_all(
        sums.reshape(plane, 512 // plane, CELLS), ("slab", "rep"), 0, 0
    )
    share = call(share_kernel, [shape(plane, 512 // plane, CELLS)], (scattered,))[0]
    parts = lax.all_to_all(share, ("slab", "rep"), 0, 0).astype(F32)
    weight_grad = jnp.transpose(parts.reshape(32, 16, CELLS)[:TAPS], (1, 0, 2)) * factor
    return (
        activated.reshape(inputs.shape),
        input_grad.reshape(inputs.shape),
        weight_grad,
    )


def solution(mesh):
    placed = (
        P(("fsdp", "rep"), "slab", None, None, None),
        P("fsdp", None, None),
        P(("fsdp", "rep"), "slab", None, None, None),
    )
    return jax.shard_map(
        local,
        mesh=mesh,
        in_specs=placed,
        out_specs=(
            P(("fsdp", "rep"), "slab", None, None, None),
            P(("fsdp", "rep"), "slab", None, None, None),
            P("fsdp", None, None),
        ),
        check_vma=False,
    )
```

```python
import functools

import jax
import jax.numpy as jnp
from jax import lax
from jax.experimental import pallas as pl
from jax.experimental.pallas import tpu as pltpu
from jax.sharding import PartitionSpec as P

F32 = jnp.float32
BF16 = jnp.bfloat16
CELLS = 256
LANES = 128
SLABS = 8
OUTS = 32
TAPS = 27
HALF = 14 * 16
ROWS = 28 * OUTS
WHOLE = SLABS * CELLS
COLUMNS = WHOLE // LANES


def tap_index(along_x, along_y, along_z):
    return (along_x * 3 + along_y) * 3 + along_z


def home(pair, core, spot_ref):
    return ((pair + 4 * core + spot_ref[0]) & 7) ^ (spot_ref[0] >> 3)


def pack_kernel(spot_ref, x_ref, u_ref, out_ref, x_own, u_own, turned, sems):
    take_u = pltpu.make_async_copy(u_ref, u_own, sems.at[0])
    takes_x = [
        pltpu.make_async_copy(x_ref.at[rows, :], x_own.at[rows, :], sems.at[1 + part])
        for part, rows in enumerate((pl.ds(0, 128), pl.ds(128, 128)))
    ]
    for take in (takes_x[0], take_u, takes_x[1]):
        take.start()
    copies = []
    for part, rows in enumerate((pl.ds(0, 128), pl.ds(128, 128))):
        takes_x[part].wait()
        for slab in range(SLABS):
            copies.append(
                pltpu.make_async_copy(
                    x_own.at[rows, :],
                    out_ref.at[slab, rows, :],
                    sems.at[4 + part * SLABS + slab],
                )
            )
            copies[-1].start()
    take_u.wait()
    by_out = jnp.transpose(u_own[...].astype(F32)).astype(BF16)
    for pair in range(SLABS):
        for core in range(2):
            start = pair * OUTS + core * 16
            turned[home(pair, core, spot_ref), core * 16 : core * 16 + 16, :] = by_out[
                start : start + 16
            ]
    last = pltpu.make_async_copy(
        turned, out_ref.at[:, pl.ds(CELLS, OUTS), :], sems.at[3]
    )
    last.start()
    for copy in copies:
        copy.wait()
    last.wait()


def lane_masks():
    lane = lax.broadcasted_iota(jnp.int32, (16, LANES), 1)
    row = (lane >> 3) & 7
    col = lane & 7
    return lane < 64, row, col


def inside(coordinate, shift):
    moved = coordinate + shift
    return (moved >= 0) & (moved < 8)


def turn(block, shift):
    return pltpu.roll(block, shift % LANES, 1)


def main_kernel(
    core_ref, r_ref, same_ref, opposite_ref, out_ref, own_ref, other_ref, g_ref, w2_ref, z_ref
):
    first = core_ref[0] == 0
    for tap in range(TAPS):
        start = tap * OUTS
        same, opposite = same_ref[tap], opposite_ref[tap]
        w2_ref[start : start + 16, :] = jnp.where(first, same, opposite)
        w2_ref[start + 16 : start + 32, :] = jnp.where(first, opposite, same)
    w2_ref[TAPS * OUTS :, :] = jnp.zeros((OUTS, CELLS), BF16)
    g_ref[TAPS * OUTS :, :] = jnp.zeros((OUTS, WHOLE), BF16)
    taps_by_outs = w2_ref[: TAPS * OUTS, :]
    for slab in range(SLABS):
        z_ref[:, slab * CELLS : (slab + 1) * CELLS] = lax.dot_general(
            taps_by_outs,
            r_ref[slab, :CELLS, :],
            (((1,), (1,)), ((), ())),
            preferred_element_type=F32,
        )
    low, row, col = lane_masks()
    zero = jnp.zeros((16, LANES), F32)
    for group in range(2):

        def term(along_x, along_y, along_z, column):
            if column < 0 or column >= COLUMNS:
                return zero
            start = tap_index(along_x, along_y, along_z) * OUTS + group * 16
            return z_ref[start : start + 16, column * LANES : (column + 1) * LANES]

        grads = []
        for column in range(COLUMNS):
            total = None
            for c in range(3):
                over_y = None
                for b in range(3):
                    mixed = jnp.where(
                        low,
                        term(2, b, c, column + 1) + term(0, b, c, column),
                        term(2, b, c, column) + term(0, b, c, column - 1),
                    )
                    over_x = term(1, b, c, column) + turn(mixed, 64)
                    if b != 1:
                        over_x = jnp.where(inside(row, b - 1), turn(over_x, -8 * (b - 1)), 0.0)
                    over_y = over_x if over_y is None else over_y + over_x
                if c != 1:
                    over_y = jnp.where(inside(col, c - 1), turn(over_y, -(c - 1)), 0.0)
                total = over_y if total is None else total + over_y
            slab, part = column // 2, column % 2
            lanes = slice(part * LANES, (part + 1) * LANES)
            logistic = 1.0 / (1.0 + jnp.exp(-total))
            out_ref[slab, CELLS + group * 16 : CELLS + group * 16 + 16, lanes] = (
                total * logistic
            ).astype(BF16)
            upstream = r_ref[
                slab, CELLS + group * 16 : CELLS + group * 16 + 16, lanes
            ].astype(F32)
            grad = upstream * (logistic * (1.0 + total * (1.0 - logistic)))
            grads.append(grad.astype(BF16).astype(F32))
        for c in range(3):
            if c == 1:
                by_z = grads
            else:
                by_z = [jnp.where(inside(col, 1 - c), turn(g, c - 1), 0.0) for g in grads]
            for b in range(3):
                if b == 1:
                    by_y = by_z
                else:
                    by_y = [
                        jnp.where(inside(row, 1 - b), turn(g, 8 * (b - 1)), 0.0) for g in by_z
                    ]
                swapped = [zero] + [turn(g, 64) for g in by_y] + [zero]
                for column in range(COLUMNS):
                    lanes = slice(column * LANES, (column + 1) * LANES)
                    here = swapped[column + 1]
                    for a, value in (
                        (0, jnp.where(low, here, swapped[column + 2])),
                        (1, by_y[column]),
                        (2, jnp.where(low, swapped[column], here)),
                    ):
                        start = tap_index(a, b, c) * OUTS + group * 16
                        g_ref[start : start + 16, lanes] = value.astype(BF16)
    whole = jnp.dot(
        g_ref[: TAPS * OUTS, :],
        r_ref[:, :CELLS, :].reshape(WHOLE, CELLS),
        preferred_element_type=F32,
    )
    own_ref[TAPS * 16 :, :] = jnp.zeros((16, CELLS), F32)
    other_ref[TAPS * 16 :, :] = jnp.zeros((16, CELLS), BF16)
    for tap in range(TAPS):
        start = tap * OUTS
        left = whole[start : start + 16]
        right = whole[start + 16 : start + 32]
        own_ref[tap * 16 : tap * 16 + 16, :] = jnp.where(first, left, right)
        other_ref[tap * 16 : tap * 16 + 16, :] = jnp.where(first, right, left).astype(
            other_ref.dtype
        )
    turned = jnp.transpose(w2_ref[...].astype(F32)).astype(BF16)
    for slab in range(SLABS):
        out_ref[slab, :CELLS, :] = jnp.dot(
            turned, g_ref[:, slab * CELLS : (slab + 1) * CELLS], preferred_element_type=F32
        ).astype(BF16)


def halve_kernel(rep_ref, own_ref, got_ref, kept_ref, sent_ref):
    first = rep_ref[0] == 0
    low = own_ref[:HALF, :] + got_ref[:HALF, :].astype(F32)
    high = own_ref[HALF:, :] + got_ref[HALF:, :].astype(F32)
    kept_ref[...] = jnp.where(first, low, high)
    sent_ref[...] = jnp.where(first, high, low).astype(BF16)


def add_kernel(kept_ref, got_ref, out_ref):
    out_ref[...] = (kept_ref[...] + got_ref[...].astype(F32)).astype(BF16)


def lengthen_kernel(rows_ref, after_ref, out_ref):
    out_ref[:HALF, :] = rows_ref[...]
    out_ref[HALF:, :] = jnp.zeros((out_ref.shape[0] - HALF, CELLS), BF16)


def share_kernel(parts_ref, out_ref):
    total = parts_ref[0].astype(F32)
    for place in range(1, parts_ref.shape[0]):
        total = total + parts_ref[place].astype(F32)
    for place in range(out_ref.shape[0]):
        out_ref[place] = total.astype(BF16)


def settle_kernel(factor, parts_ref, out_ref):
    for tap in range(TAPS):
        rep, place = tap // 14, tap % 14
        rows = slice(place % 2 * 16, place % 2 * 16 + 16)
        out_ref[tap] = parts_ref[place // 2 * 2 + rep, rows, :].astype(F32) * factor


def final_kernel(spot_ref, r_ref, act_ref, grad_ref):
    total = r_ref[0, :CELLS, :].astype(F32)
    for slab in range(1, SLABS):
        total = total + r_ref[slab, :CELLS, :].astype(F32)
    grad_ref[...] = jnp.transpose(total).astype(BF16)
    for half in range(2):
        turned = jnp.transpose(
            jnp.concatenate(
                [
                    r_ref[
                        home(pair, core, spot_ref),
                        CELLS + core * 16 : CELLS + core * 16 + 16,
                        :,
                    ].astype(F32)
                    for pair in range(half * 4, half * 4 + 4)
                    for core in range(2)
                ],
                axis=0,
            )
        )
        act_ref[:, half * LANES : (half + 1) * LANES] = turned.astype(BF16)


VMEM = pl.BlockSpec(memory_space=pltpu.VMEM)
SMEM = pl.BlockSpec(memory_space=pltpu.SMEM)
ANY = pl.BlockSpec(memory_space=pl.ANY)
HBM = pl.BlockSpec(memory_space=pltpu.HBM)


def shape(*dims, dtype=BF16):
    return jax.ShapeDtypeStruct(dims, dtype)


def call(kernel, outs, operands, specs=None, scratch=(), flops=0, out_spec=VMEM, vmem=48):
    moved = sum(a.size * a.dtype.itemsize for a in list(operands) + list(outs))
    return pl.pallas_call(
        kernel,
        out_shape=tuple(outs),
        in_specs=specs or [VMEM] * len(operands),
        out_specs=tuple(out_spec for _ in outs),
        scratch_shapes=list(scratch),
        compiler_params=pltpu.CompilerParams(vmem_limit_bytes=vmem * 1024 * 1024),
        cost_estimate=pl.CostEstimate(flops=flops, bytes_accessed=moved, transcendentals=0),
    )(*operands)


def local(inputs, weights, upstream):
    owner = lax.axis_index("fsdp")
    core = (owner % 2).astype(jnp.int32).reshape(1)
    rep = lax.axis_index("rep").astype(jnp.int32).reshape(1)
    spot = (owner // 2 + 8 * lax.axis_index("rep")).astype(jnp.int32).reshape(1)
    chips = lax.axis_size("fsdp") // 2
    reps = lax.axis_size("rep")
    total_cells = 2 * chips * reps * WHOLE
    factor = float(total_cells) ** (-0.5)

    def place(z, core, y, rep):
        return ((z * 2 + core) * SLABS + y) * reps + rep

    everyone = ("fsdp", "slab", "rep")
    mirrored = [
        (place(z, core, y, rep), place(((y ^ rep) + 4 * core - z) % SLABS, core, y, rep))
        for z in range(chips)
        for core in range(2)
        for y in range(SLABS)
        for rep in range(reps)
    ]
    cores = [(2 * z + core, 2 * z + 1 - core) for z in range(chips) for core in range(2)]

    by_tap = jnp.transpose(weights, (1, 0, 2))
    same = lax.ppermute(by_tap, everyone, mirrored)
    opposite = lax.ppermute(same, "fsdp", cores)

    cells = inputs.reshape(CELLS, CELLS)
    packed = call(
        pack_kernel,
        [shape(SLABS, CELLS + OUTS, CELLS)],
        (spot, cells, upstream.reshape(CELLS, CELLS)),
        specs=[SMEM, HBM, HBM],
        scratch=[
            pltpu.VMEM((CELLS, CELLS), BF16),
            pltpu.VMEM((CELLS, CELLS), BF16),
            pltpu.VMEM((SLABS, OUTS, CELLS), BF16),
            pltpu.SemaphoreType.DMA((4 + 2 * SLABS,)),
        ],
        out_spec=HBM,
        vmem=56,
    )[0]
    gathered = lax.all_to_all(packed, "slab", 0, 0)

    terms, own, other = call(
        main_kernel,
        [
            shape(SLABS, CELLS + OUTS, CELLS),
            shape(2 * HALF, CELLS, dtype=F32),
            shape(2 * HALF, CELLS),
        ],
        (core, gathered, same, opposite),
        specs=[SMEM, VMEM, VMEM, VMEM],
        scratch=[
            pltpu.VMEM((ROWS, WHOLE), BF16),
            pltpu.VMEM((ROWS, CELLS), BF16),
            pltpu.VMEM((TAPS * OUTS, WHOLE), F32),
        ],
        flops=6 * ROWS * WHOLE * CELLS,
    )
    returned = lax.all_to_all(terms, "slab", 0, 0)
    activated, input_grad = call(
        final_kernel,
        [shape(CELLS, CELLS), shape(CELLS, CELLS)],
        (spot, returned),
        specs=[SMEM, VMEM],
    )

    kept, sent = call(
        halve_kernel,
        [shape(HALF, CELLS, dtype=F32), shape(HALF, CELLS)],
        (rep, own, lax.ppermute(other, "fsdp", cores)),
        specs=[SMEM, VMEM, VMEM],
    )
    beside = [
        (place(z, core, y, rep), place(z, core, y ^ 1, 1 - rep))
        for z in range(chips)
        for core in range(2)
        for y in range(SLABS)
        for rep in range(reps)
    ]
    got = lax.ppermute(sent, everyone, beside)
    sums = call(add_kernel, [shape(HALF, CELLS)], (kept, got))[0]
    sums = lax.ppermute(sums, everyone, mirrored)
    sums = call(lengthen_kernel, [shape(256, CELLS)], (sums, returned), specs=[VMEM, ANY])[0]
    scattered = lax.all_to_all(sums.reshape(SLABS, 32, CELLS), "slab", 0, 0)
    share = call(share_kernel, [shape(SLABS * reps, 32, CELLS)], (scattered,))[0]
    parts = lax.all_to_all(share, ("slab", "rep"), 0, 0)
    weight_grad = call(
        functools.partial(settle_kernel, factor),
        [shape(TAPS, 16, CELLS, dtype=F32)],
        (parts,),
    )[0]
    weight_grad = jnp.transpose(weight_grad, (1, 0, 2))
    return (
        activated.reshape(inputs.shape),
        input_grad.reshape(inputs.shape),
        weight_grad,
    )


def solution(mesh):
    placed = (
        P(("fsdp", "rep"), "slab", None, None, None),
        P("fsdp", None, None),
        P(("fsdp", "rep"), "slab", None, None, None),
    )
    return jax.shard_map(
        local,
        mesh=mesh,
        in_specs=placed,
        out_specs=(
            P(("fsdp", "rep"), "slab", None, None, None),
            P(("fsdp", "rep"), "slab", None, None, None),
            P("fsdp", None, None),
        ),
        check_vma=False,
    )
```

```python
import jax
import jax.numpy as jnp
from jax import lax
from jax.experimental import pallas as pl
from jax.experimental.pallas import tpu as pltpu
from jax.sharding import PartitionSpec as P

F32 = jnp.float32
BF16 = jnp.bfloat16
CELLS = 256
LANES = 128
SLABS = 8
OUTS = 32
TAPS = 27
ROWS = 28 * OUTS
WHOLE = SLABS * CELLS
COLUMNS = WHOLE // LANES


def tap_index(along_x, along_y, along_z):
    return (along_x * 3 + along_y) * 3 + along_z


def home(pair, core, spot_ref):
    return ((pair + 4 * core + spot_ref[0]) & 7) ^ (spot_ref[0] >> 3)


def pack_kernel(spot_ref, x_ref, u_ref, out_ref, x_own, u_own, turned, sems):
    take_u = pltpu.make_async_copy(u_ref, u_own, sems.at[0])
    takes_x = [
        pltpu.make_async_copy(x_ref.at[rows, :], x_own.at[rows, :], sems.at[1 + part])
        for part, rows in enumerate((pl.ds(0, 128), pl.ds(128, 128)))
    ]
    for take in (takes_x[0], take_u, takes_x[1]):
        take.start()
    copies = []
    for part, rows in enumerate((pl.ds(0, 128), pl.ds(128, 128))):
        takes_x[part].wait()
        for slab in range(SLABS):
            copies.append(
                pltpu.make_async_copy(
                    x_own.at[rows, :],
                    out_ref.at[slab, rows, :],
                    sems.at[4 + part * SLABS + slab],
                )
            )
            copies[-1].start()
    take_u.wait()
    by_out = jnp.transpose(u_own[...].astype(F32)).astype(BF16)
    for pair in range(SLABS):
        for core in range(2):
            start = pair * OUTS + core * 16
            turned[home(pair, core, spot_ref), core * 16 : core * 16 + 16, :] = by_out[
                start : start + 16
            ]
    last = pltpu.make_async_copy(
        turned, out_ref.at[:, pl.ds(CELLS, OUTS), :], sems.at[3]
    )
    last.start()
    for copy in copies:
        copy.wait()
    last.wait()


def lane_masks():
    lane = lax.broadcasted_iota(jnp.int32, (16, LANES), 1)
    row = (lane >> 3) & 7
    col = lane & 7
    return lane < 64, row, col


def inside(coordinate, shift):
    moved = coordinate + shift
    return (moved >= 0) & (moved < 8)


def turn(block, shift):
    return pltpu.roll(block, shift % LANES, 1)


def main_kernel(
    corner_ref,
    r_ref,
    mine_ref,
    got_ref,
    mine_opposite_ref,
    got_opposite_ref,
    out_ref,
    own_ref,
    other_ref,
    g_ref,
    w2_ref,
    z_ref,
):
    first = (corner_ref[0] & 1) == 0
    lower = corner_ref[0] < 2
    for tap in range(TAPS):
        start = tap * OUTS
        place = tap if tap < 14 else tap - 13
        leads = lower if tap < 14 else jnp.logical_not(lower)
        same = jnp.where(leads, mine_ref[place], got_ref[place])
        opposite = jnp.where(leads, mine_opposite_ref[place], got_opposite_ref[place])
        w2_ref[start : start + 16, :] = jnp.where(first, same, opposite)
        w2_ref[start + 16 : start + 32, :] = jnp.where(first, opposite, same)
    w2_ref[TAPS * OUTS :, :] = jnp.zeros((OUTS, CELLS), BF16)
    g_ref[TAPS * OUTS :, :] = jnp.zeros((OUTS, WHOLE), BF16)
    taps_by_outs = w2_ref[: TAPS * OUTS, :]
    for slab in range(SLABS):
        z_ref[:, slab * CELLS : (slab + 1) * CELLS] = lax.dot_general(
            taps_by_outs,
            r_ref[slab, :CELLS, :],
            (((1,), (1,)), ((), ())),
            preferred_element_type=F32,
        )
    low, row, col = lane_masks()
    zero = jnp.zeros((16, LANES), F32)
    for group in range(2):

        def term(along_x, along_y, along_z, column):
            if column < 0 or column >= COLUMNS:
                return zero
            start = tap_index(along_x, along_y, along_z) * OUTS + group * 16
            return z_ref[start : start + 16, column * LANES : (column + 1) * LANES]

        grads = []
        for column in range(COLUMNS):
            total = None
            for c in range(3):
                over_y = None
                for b in range(3):
                    mixed = jnp.where(
                        low,
                        term(2, b, c, column + 1) + term(0, b, c, column),
                        term(2, b, c, column) + term(0, b, c, column - 1),
                    )
                    over_x = term(1, b, c, column) + turn(mixed, 64)
                    if b != 1:
                        over_x = jnp.where(inside(row, b - 1), turn(over_x, -8 * (b - 1)), 0.0)
                    over_y = over_x if over_y is None else over_y + over_x
                if c != 1:
                    over_y = jnp.where(inside(col, c - 1), turn(over_y, -(c - 1)), 0.0)
                total = over_y if total is None else total + over_y
            slab, part = column // 2, column % 2
            lanes = slice(part * LANES, (part + 1) * LANES)
            logistic = 1.0 / (1.0 + jnp.exp(-total))
            out_ref[slab, CELLS + group * 16 : CELLS + group * 16 + 16, lanes] = (
                total * logistic
            ).astype(BF16)
            upstream = r_ref[
                slab, CELLS + group * 16 : CELLS + group * 16 + 16, lanes
            ].astype(F32)
            grad = upstream * (logistic * (1.0 + total * (1.0 - logistic)))
            grads.append(grad.astype(BF16).astype(F32))
        for c in range(3):
            if c == 1:
                by_z = grads
            else:
                by_z = [jnp.where(inside(col, 1 - c), turn(g, c - 1), 0.0) for g in grads]
            for b in range(3):
                if b == 1:
                    by_y = by_z
                else:
                    by_y = [
                        jnp.where(inside(row, 1 - b), turn(g, 8 * (b - 1)), 0.0) for g in by_z
                    ]
                swapped = [zero] + [turn(g, 64) for g in by_y] + [zero]
                for column in range(COLUMNS):
                    lanes = slice(column * LANES, (column + 1) * LANES)
                    here = swapped[column + 1]
                    for a, value in (
                        (0, jnp.where(low, here, swapped[column + 2])),
                        (1, by_y[column]),
                        (2, jnp.where(low, swapped[column], here)),
                    ):
                        start = tap_index(a, b, c) * OUTS + group * 16
                        g_ref[start : start + 16, lanes] = value.astype(BF16)
    whole = jnp.dot(
        g_ref[: TAPS * OUTS, :],
        r_ref[:, :CELLS, :].reshape(WHOLE, CELLS),
        preferred_element_type=F32,
    )
    for tap in range(TAPS):
        start = tap * OUTS
        left = whole[start : start + 16]
        right = whole[start + 16 : start + 32]
        own_ref[tap * 16 : tap * 16 + 16, :] = jnp.where(first, left, right)
        other_ref[tap * 16 : tap * 16 + 16, :] = jnp.where(first, right, left).astype(BF16)
    turned = jnp.transpose(w2_ref[...].astype(F32)).astype(BF16)
    for slab in range(SLABS):
        out_ref[slab, :CELLS, :] = jnp.dot(
            turned, g_ref[:, slab * CELLS : (slab + 1) * CELLS], preferred_element_type=F32
        ).astype(BF16)


def add_kernel(own_ref, got_ref, out_ref):
    out_ref[...] = (own_ref[...] + got_ref[...].astype(F32)).astype(BF16)


def lengthen_kernel(rows_ref, after_ref, out_ref):
    out_ref[: TAPS * 16, :] = rows_ref[...]
    out_ref[TAPS * 16 :, :] = jnp.zeros((out_ref.shape[0] - TAPS * 16, CELLS), BF16)


def share_kernel(parts_ref, out_ref):
    total = parts_ref[0].astype(F32)
    for place in range(1, parts_ref.shape[0]):
        total = total + parts_ref[place].astype(F32)
    for place in range(out_ref.shape[0]):
        out_ref[place] = total.astype(BF16)


def final_kernel(spot_ref, r_ref, act_ref, grad_ref):
    total = r_ref[0, :CELLS, :].astype(F32)
    for slab in range(1, SLABS):
        total = total + r_ref[slab, :CELLS, :].astype(F32)
    grad_ref[...] = jnp.transpose(total).astype(BF16)
    for half in range(2):
        turned = jnp.transpose(
            jnp.concatenate(
                [
                    r_ref[
                        home(pair, core, spot_ref),
                        CELLS + core * 16 : CELLS + core * 16 + 16,
                        :,
                    ].astype(F32)
                    for pair in range(half * 4, half * 4 + 4)
                    for core in range(2)
                ],
                axis=0,
            )
        )
        act_ref[:, half * LANES : (half + 1) * LANES] = turned.astype(BF16)


VMEM = pl.BlockSpec(memory_space=pltpu.VMEM)
SMEM = pl.BlockSpec(memory_space=pltpu.SMEM)
ANY = pl.BlockSpec(memory_space=pl.ANY)
HBM = pl.BlockSpec(memory_space=pltpu.HBM)


def shape(*dims, dtype=BF16):
    return jax.ShapeDtypeStruct(dims, dtype)


def call(kernel, outs, operands, specs=None, scratch=(), flops=0, out_spec=VMEM, vmem=48):
    moved = sum(a.size * a.dtype.itemsize for a in list(operands) + list(outs))
    return pl.pallas_call(
        kernel,
        out_shape=tuple(outs),
        in_specs=specs or [VMEM] * len(operands),
        out_specs=tuple(out_spec for _ in outs),
        scratch_shapes=list(scratch),
        compiler_params=pltpu.CompilerParams(vmem_limit_bytes=vmem * 1024 * 1024),
        cost_estimate=pl.CostEstimate(flops=flops, bytes_accessed=moved, transcendentals=0),
    )(*operands)


def local(inputs, weights, upstream):
    owner = lax.axis_index("fsdp")
    rep_here = lax.axis_index("rep")
    corner = (owner % 2 + 2 * rep_here).astype(jnp.int32).reshape(1)
    spot = (owner // 2 + 8 * rep_here).astype(jnp.int32).reshape(1)
    chips = lax.axis_size("fsdp") // 2
    reps = lax.axis_size("rep")
    total_cells = 2 * chips * reps * WHOLE
    factor = float(total_cells) ** (-0.5)

    def place(z, core, y, rep):
        return ((z * 2 + core) * SLABS + y) * reps + rep

    everyone = ("fsdp", "slab", "rep")
    mirrored = [
        (place(z, core, y, rep), place(((y ^ rep) + 4 * core - z) % SLABS, core, y, rep))
        for z in range(chips)
        for core in range(2)
        for y in range(SLABS)
        for rep in range(reps)
    ]
    cores = [(2 * z + core, 2 * z + 1 - core) for z in range(chips) for core in range(2)]

    by_tap = jnp.transpose(weights, (1, 0, 2))
    beside = [
        (place(z, core, y, rep), place(z, core, y ^ 1, 1 - rep))
        for z in range(chips)
        for core in range(2)
        for y in range(SLABS)
        for rep in range(reps)
    ]
    mine = lax.dynamic_slice_in_dim(by_tap, 13 * rep_here, 14, axis=0)
    mine = lax.ppermute(mine, everyone, mirrored)
    got = lax.ppermute(mine, everyone, beside)
    halves = (mine, got, lax.ppermute(mine, "fsdp", cores), lax.ppermute(got, "fsdp", cores))

    cells = inputs.reshape(CELLS, CELLS)
    packed = call(
        pack_kernel,
        [shape(SLABS, CELLS + OUTS, CELLS)],
        (spot, cells, upstream.reshape(CELLS, CELLS)),
        specs=[SMEM, HBM, HBM],
        scratch=[
            pltpu.VMEM((CELLS, CELLS), BF16),
            pltpu.VMEM((CELLS, CELLS), BF16),
            pltpu.VMEM((SLABS, OUTS, CELLS), BF16),
            pltpu.SemaphoreType.DMA((4 + 2 * SLABS,)),
        ],
        out_spec=HBM,
        vmem=56,
    )[0]
    gathered = lax.all_to_all(packed, "slab", 0, 0)

    terms, own, other = call(
        main_kernel,
        [
            shape(SLABS, CELLS + OUTS, CELLS),
            shape(TAPS * 16, CELLS, dtype=F32),
            shape(TAPS * 16, CELLS),
        ],
        (corner, gathered, *halves),
        specs=[SMEM] + [VMEM] * 5,
        scratch=[
            pltpu.VMEM((ROWS, WHOLE), BF16),
            pltpu.VMEM((ROWS, CELLS), BF16),
            pltpu.VMEM((TAPS * OUTS, WHOLE), F32),
        ],
        flops=6 * ROWS * WHOLE * CELLS,
    )
    returned = lax.all_to_all(terms, "slab", 0, 0)
    activated, input_grad = call(
        final_kernel,
        [shape(CELLS, CELLS), shape(CELLS, CELLS)],
        (spot, returned),
        specs=[SMEM, VMEM],
    )

    sums = call(
        add_kernel, [shape(TAPS * 16, CELLS)], (own, lax.ppermute(other, "fsdp", cores))
    )[0]
    sums = lax.ppermute(sums, everyone, mirrored)
    plane = SLABS * reps
    sums = call(
        lengthen_kernel,
        [shape(512, CELLS)],
        (sums, returned),
        specs=[VMEM, ANY],
    )[0]
    scattered = lax.all_to_all(
        sums.reshape(plane, 512 // plane, CELLS), ("slab", "rep"), 0, 0
    )
    share = call(share_kernel, [shape(plane, 512 // plane, CELLS)], (scattered,))[0]
    parts = lax.all_to_all(share, ("slab", "rep"), 0, 0).astype(F32)
    weight_grad = jnp.transpose(parts.reshape(32, 16, CELLS)[:TAPS], (1, 0, 2)) * factor
    return (
        activated.reshape(inputs.shape),
        input_grad.reshape(inputs.shape),
        weight_grad,
    )


def solution(mesh):
    placed = (
        P(("fsdp", "rep"), "slab", None, None, None),
        P("fsdp", None, None),
        P(("fsdp", "rep"), "slab", None, None, None),
    )
    return jax.shard_map(
        local,
        mesh=mesh,
        in_specs=placed,
        out_specs=(
            P(("fsdp", "rep"), "slab", None, None, None),
            P(("fsdp", "rep"), "slab", None, None, None),
            P("fsdp", None, None),
        ),
        check_vma=False,
    )
```

```python
import jax
import jax.numpy as jnp
from jax import lax
from jax.experimental import pallas as pl
from jax.experimental.pallas import tpu as pltpu
from jax.sharding import PartitionSpec as P

F32 = jnp.float32
BF16 = jnp.bfloat16
CELLS = 256
LANES = 128
SLABS = 8
OUTS = 32
TAPS = 27
ROWS = 28 * OUTS
WHOLE = SLABS * CELLS
COLUMNS = WHOLE // LANES


def tap_index(along_x, along_y, along_z):
    return (along_x * 3 + along_y) * 3 + along_z


def home(pair, core, chip):
    return (pair + 4 * core + chip) & 7


def pack_kernel(chip_ref, x_ref, u_ref, out_ref, x_own, u_own, turned, sems):
    take_u = pltpu.make_async_copy(u_ref, u_own, sems.at[0])
    takes_x = [
        pltpu.make_async_copy(x_ref.at[rows, :], x_own.at[rows, :], sems.at[1 + part])
        for part, rows in enumerate((pl.ds(0, 128), pl.ds(128, 128)))
    ]
    for take in (takes_x[0], take_u, takes_x[1]):
        take.start()
    copies = []
    for part, rows in enumerate((pl.ds(0, 128), pl.ds(128, 128))):
        takes_x[part].wait()
        for slab in range(SLABS):
            copies.append(
                pltpu.make_async_copy(
                    x_own.at[rows, :],
                    out_ref.at[slab, rows, :],
                    sems.at[4 + part * SLABS + slab],
                )
            )
            copies[-1].start()
    take_u.wait()
    by_out = jnp.transpose(u_own[...].astype(F32)).astype(BF16)
    for pair in range(SLABS):
        for core in range(2):
            start = pair * OUTS + core * 16
            turned[home(pair, core, chip_ref[0]), core * 16 : core * 16 + 16, :] = by_out[
                start : start + 16
            ]
    last = pltpu.make_async_copy(
        turned, out_ref.at[:, pl.ds(CELLS, OUTS), :], sems.at[3]
    )
    last.start()
    for copy in copies:
        copy.wait()
    last.wait()


def lane_masks():
    lane = lax.broadcasted_iota(jnp.int32, (16, LANES), 1)
    row = (lane >> 3) & 7
    col = lane & 7
    return lane < 64, row, col


def inside(coordinate, shift):
    moved = coordinate + shift
    return (moved >= 0) & (moved < 8)


def turn(block, shift):
    return pltpu.roll(block, shift % LANES, 1)


def main_kernel(
    core_ref, r_ref, same_ref, opposite_ref, out_ref, own_ref, other_ref, g_ref, w2_ref, z_ref
):
    first = core_ref[0] == 0
    for tap in range(TAPS):
        start = tap * OUTS
        same, opposite = same_ref[tap], opposite_ref[tap]
        w2_ref[start : start + 16, :] = jnp.where(first, same, opposite)
        w2_ref[start + 16 : start + 32, :] = jnp.where(first, opposite, same)
    w2_ref[TAPS * OUTS :, :] = jnp.zeros((OUTS, CELLS), BF16)
    g_ref[TAPS * OUTS :, :] = jnp.zeros((OUTS, WHOLE), BF16)
    taps_by_outs = w2_ref[: TAPS * OUTS, :]
    for slab in range(SLABS):
        z_ref[:, slab * CELLS : (slab + 1) * CELLS] = lax.dot_general(
            taps_by_outs,
            r_ref[slab, :CELLS, :],
            (((1,), (1,)), ((), ())),
            preferred_element_type=F32,
        )
    low, row, col = lane_masks()
    zero = jnp.zeros((16, LANES), F32)
    for group in range(2):

        def term(along_x, along_y, along_z, column):
            if column < 0 or column >= COLUMNS:
                return zero
            start = tap_index(along_x, along_y, along_z) * OUTS + group * 16
            return z_ref[start : start + 16, column * LANES : (column + 1) * LANES]

        grads = []
        for column in range(COLUMNS):
            total = None
            for c in range(3):
                over_y = None
                for b in range(3):
                    mixed = jnp.where(
                        low,
                        term(2, b, c, column + 1) + term(0, b, c, column),
                        term(2, b, c, column) + term(0, b, c, column - 1),
                    )
                    over_x = term(1, b, c, column) + turn(mixed, 64)
                    if b != 1:
                        over_x = jnp.where(inside(row, b - 1), turn(over_x, -8 * (b - 1)), 0.0)
                    over_y = over_x if over_y is None else over_y + over_x
                if c != 1:
                    over_y = jnp.where(inside(col, c - 1), turn(over_y, -(c - 1)), 0.0)
                total = over_y if total is None else total + over_y
            slab, part = column // 2, column % 2
            lanes = slice(part * LANES, (part + 1) * LANES)
            logistic = 1.0 / (1.0 + jnp.exp(-total))
            out_ref[slab, CELLS + group * 16 : CELLS + group * 16 + 16, lanes] = (
                total * logistic
            ).astype(BF16)
            upstream = r_ref[
                slab, CELLS + group * 16 : CELLS + group * 16 + 16, lanes
            ].astype(F32)
            grad = upstream * (logistic * (1.0 + total * (1.0 - logistic)))
            grads.append(grad.astype(BF16).astype(F32))
        for c in range(3):
            if c == 1:
                by_z = grads
            else:
                by_z = [jnp.where(inside(col, 1 - c), turn(g, c - 1), 0.0) for g in grads]
            for b in range(3):
                if b == 1:
                    by_y = by_z
                else:
                    by_y = [
                        jnp.where(inside(row, 1 - b), turn(g, 8 * (b - 1)), 0.0) for g in by_z
                    ]
                swapped = [zero] + [turn(g, 64) for g in by_y] + [zero]
                for column in range(COLUMNS):
                    lanes = slice(column * LANES, (column + 1) * LANES)
                    here = swapped[column + 1]
                    for a, value in (
                        (0, jnp.where(low, here, swapped[column + 2])),
                        (1, by_y[column]),
                        (2, jnp.where(low, swapped[column], here)),
                    ):
                        start = tap_index(a, b, c) * OUTS + group * 16
                        g_ref[start : start + 16, lanes] = value.astype(BF16)
    whole = jnp.dot(
        g_ref[: TAPS * OUTS, :],
        r_ref[:, :CELLS, :].reshape(WHOLE, CELLS),
        preferred_element_type=F32,
    )
    for tap in range(TAPS):
        start = tap * OUTS
        left = whole[start : start + 16]
        right = whole[start + 16 : start + 32]
        own_ref[tap * 16 : tap * 16 + 16, :] = jnp.where(first, left, right)
        other_ref[tap * 16 : tap * 16 + 16, :] = jnp.where(first, right, left).astype(BF16)
    turned = jnp.transpose(w2_ref[...].astype(F32)).astype(BF16)
    for slab in range(SLABS):
        out_ref[slab, :CELLS, :] = jnp.dot(
            turned, g_ref[:, slab * CELLS : (slab + 1) * CELLS], preferred_element_type=F32
        ).astype(BF16)


def add_kernel(own_ref, got_ref, out_ref):
    out_ref[...] = (own_ref[...] + got_ref[...].astype(F32)).astype(BF16)


def lengthen_kernel(rows_ref, after_ref, out_ref):
    rows = out_ref.shape[1]
    reps = out_ref.shape[0] // SLABS
    for slab in range(SLABS):
        held = max(0, min(rows, TAPS * 16 - slab * rows))
        for rep in range(reps):
            place = slab * reps + rep
            if held > 0:
                out_ref[place, :held, :] = rows_ref[slab * rows : slab * rows + held, :]
            if held < rows:
                out_ref[place, held:, :] = jnp.zeros((rows - held, CELLS), BF16)


def share_kernel(parts_ref, out_ref):
    total = parts_ref[0].astype(F32)
    for place in range(1, parts_ref.shape[0]):
        total = total + parts_ref[place].astype(F32)
    for place in range(out_ref.shape[0]):
        out_ref[place] = total.astype(BF16)


def final_kernel(chip_ref, r_ref, act_ref, grad_ref):
    total = r_ref[0, :CELLS, :].astype(F32)
    for slab in range(1, SLABS):
        total = total + r_ref[slab, :CELLS, :].astype(F32)
    grad_ref[...] = jnp.transpose(total).astype(BF16)
    for half in range(2):
        turned = jnp.transpose(
            jnp.concatenate(
                [
                    r_ref[
                        home(pair, core, chip_ref[0]),
                        CELLS + core * 16 : CELLS + core * 16 + 16,
                        :,
                    ].astype(F32)
                    for pair in range(half * 4, half * 4 + 4)
                    for core in range(2)
                ],
                axis=0,
            )
        )
        act_ref[:, half * LANES : (half + 1) * LANES] = turned.astype(BF16)


VMEM = pl.BlockSpec(memory_space=pltpu.VMEM)
SMEM = pl.BlockSpec(memory_space=pltpu.SMEM)
ANY = pl.BlockSpec(memory_space=pl.ANY)
HBM = pl.BlockSpec(memory_space=pltpu.HBM)


def shape(*dims, dtype=BF16):
    return jax.ShapeDtypeStruct(dims, dtype)


def call(kernel, outs, operands, specs=None, scratch=(), flops=0, out_spec=VMEM, vmem=48):
    moved = sum(a.size * a.dtype.itemsize for a in list(operands) + list(outs))
    return pl.pallas_call(
        kernel,
        out_shape=tuple(outs),
        in_specs=specs or [VMEM] * len(operands),
        out_specs=tuple(out_spec for _ in outs),
        scratch_shapes=list(scratch),
        compiler_params=pltpu.CompilerParams(vmem_limit_bytes=vmem * 1024 * 1024),
        cost_estimate=pl.CostEstimate(flops=flops, bytes_accessed=moved, transcendentals=0),
    )(*operands)


def local(inputs, weights, upstream):
    owner = lax.axis_index("fsdp")
    core = (owner % 2).astype(jnp.int32).reshape(1)
    chip = (owner // 2).astype(jnp.int32).reshape(1)
    chips = lax.axis_size("fsdp") // 2
    reps = lax.axis_size("rep")
    total_cells = 2 * chips * reps * WHOLE
    factor = float(total_cells) ** (-0.5)

    def place(z, core, y, rep):
        return ((z * 2 + core) * SLABS + y) * reps + rep

    everyone = ("fsdp", "slab", "rep")
    mirrored = [
        (place(z, core, y, rep), place((y + 4 * core - z) % SLABS, core, y, rep))
        for z in range(chips)
        for core in range(2)
        for y in range(SLABS)
        for rep in range(reps)
    ]
    cores = [(2 * z + core, 2 * z + 1 - core) for z in range(chips) for core in range(2)]

    by_tap = jnp.transpose(weights, (1, 0, 2))
    same = lax.ppermute(by_tap, everyone, mirrored)
    opposite = lax.ppermute(same, "fsdp", cores)

    cells = inputs.reshape(CELLS, CELLS)
    packed = call(
        pack_kernel,
        [shape(SLABS, CELLS + OUTS, CELLS)],
        (chip, cells, upstream.reshape(CELLS, CELLS)),
        specs=[SMEM, HBM, HBM],
        scratch=[
            pltpu.VMEM((CELLS, CELLS), BF16),
            pltpu.VMEM((CELLS, CELLS), BF16),
            pltpu.VMEM((SLABS, OUTS, CELLS), BF16),
            pltpu.SemaphoreType.DMA((4 + 2 * SLABS,)),
        ],
        out_spec=HBM,
        vmem=56,
    )[0]
    gathered = lax.all_to_all(packed, "slab", 0, 0)

    terms, own, other = call(
        main_kernel,
        [
            shape(SLABS, CELLS + OUTS, CELLS),
            shape(TAPS * 16, CELLS, dtype=F32),
            shape(TAPS * 16, CELLS),
        ],
        (core, gathered, same, opposite),
        specs=[SMEM, VMEM, VMEM, VMEM],
        scratch=[
            pltpu.VMEM((ROWS, WHOLE), BF16),
            pltpu.VMEM((ROWS, CELLS), BF16),
            pltpu.VMEM((TAPS * OUTS, WHOLE), F32),
        ],
        flops=6 * ROWS * WHOLE * CELLS,
    )
    returned = lax.all_to_all(terms, "slab", 0, 0)
    activated, input_grad = call(
        final_kernel,
        [shape(CELLS, CELLS), shape(CELLS, CELLS)],
        (chip, returned),
        specs=[SMEM, VMEM],
    )

    sums = call(
        add_kernel, [shape(TAPS * 16, CELLS)], (own, lax.ppermute(other, "fsdp", cores))
    )[0]
    sums = lax.ppermute(sums, everyone, mirrored)
    plane = SLABS * reps
    sums = call(
        lengthen_kernel, [shape(plane, 64, CELLS)], (sums, returned), specs=[VMEM, ANY]
    )[0]
    scattered = lax.all_to_all(sums, ("slab", "rep"), 0, 0)
    share = call(share_kernel, [shape(SLABS, 64, CELLS)], (scattered,))[0]
    parts = lax.all_to_all(share, "slab", 0, 0).astype(F32)
    weight_grad = jnp.transpose(parts.reshape(32, 16, CELLS)[:TAPS], (1, 0, 2)) * factor
    return (
        activated.reshape(inputs.shape),
        input_grad.reshape(inputs.shape),
        weight_grad,
    )


def solution(mesh):
    placed = (
        P(("fsdp", "rep"), "slab", None, None, None),
        P("fsdp", None, None),
        P(("fsdp", "rep"), "slab", None, None, None),
    )
    return jax.shard_map(
        local,
        mesh=mesh,
        in_specs=placed,
        out_specs=(
            P(("fsdp", "rep"), "slab", None, None, None),
            P(("fsdp", "rep"), "slab", None, None, None),
            P("fsdp", None, None),
        ),
        check_vma=False,
    )
```

```python
import jax
import jax.numpy as jnp
from jax import lax
from jax.experimental import pallas as pl
from jax.experimental.pallas import tpu as pltpu
from jax.sharding import PartitionSpec as P

F32 = jnp.float32
BF16 = jnp.bfloat16
CELLS = 256
LANES = 128
SLABS = 8
OUTS = 32
TAPS = 27
ROWS = 28 * OUTS
WHOLE = SLABS * CELLS
COLUMNS = WHOLE // LANES
AHEAD = 2 * 10**10


def tap_index(along_x, along_y, along_z):
    return (along_x * 3 + along_y) * 3 + along_z


def home(pair, core, chip):
    return (pair + 4 * core + chip) & 7


def pack_kernel(chip_ref, x_ref, u_ref, out_ref, x_own, u_own, turned, sems):
    take_u = pltpu.make_async_copy(u_ref, u_own, sems.at[0])
    takes_x = [
        pltpu.make_async_copy(x_ref.at[rows, :], x_own.at[rows, :], sems.at[1 + part])
        for part, rows in enumerate((pl.ds(0, 128), pl.ds(128, 128)))
    ]
    for take in (takes_x[0], take_u, takes_x[1]):
        take.start()
    copies = []
    for part, rows in enumerate((pl.ds(0, 128), pl.ds(128, 128))):
        takes_x[part].wait()
        for slab in range(SLABS):
            copies.append(
                pltpu.make_async_copy(
                    x_own.at[rows, :],
                    out_ref.at[slab, rows, :],
                    sems.at[4 + part * SLABS + slab],
                )
            )
            copies[-1].start()
    take_u.wait()
    by_out = jnp.transpose(u_own[...].astype(F32)).astype(BF16)
    for pair in range(SLABS):
        for core in range(2):
            start = pair * OUTS + core * 16
            turned[home(pair, core, chip_ref[0]), core * 16 : core * 16 + 16, :] = by_out[
                start : start + 16
            ]
    last = pltpu.make_async_copy(
        turned, out_ref.at[:, pl.ds(CELLS, OUTS), :], sems.at[3]
    )
    last.start()
    for copy in copies:
        copy.wait()
    last.wait()


def lane_masks():
    lane = lax.broadcasted_iota(jnp.int32, (16, LANES), 1)
    row = (lane >> 3) & 7
    col = lane & 7
    return lane < 64, row, col


def inside(coordinate, shift):
    moved = coordinate + shift
    return (moved >= 0) & (moved < 8)


def turn(block, shift):
    return pltpu.roll(block, shift % LANES, 1)


def main_kernel(
    core_ref, r_ref, same_ref, opposite_ref, out_ref, own_ref, other_ref, g_ref, w2_ref, z_ref
):
    first = core_ref[0] == 0
    for tap in range(TAPS):
        start = tap * OUTS
        same, opposite = same_ref[tap], opposite_ref[tap]
        w2_ref[start : start + 16, :] = jnp.where(first, same, opposite)
        w2_ref[start + 16 : start + 32, :] = jnp.where(first, opposite, same)
    w2_ref[TAPS * OUTS :, :] = jnp.zeros((OUTS, CELLS), BF16)
    g_ref[TAPS * OUTS :, :] = jnp.zeros((OUTS, WHOLE), BF16)
    taps_by_outs = w2_ref[: TAPS * OUTS, :]
    for slab in range(SLABS):
        z_ref[:, slab * CELLS : (slab + 1) * CELLS] = lax.dot_general(
            taps_by_outs,
            r_ref[slab, :CELLS, :],
            (((1,), (1,)), ((), ())),
            preferred_element_type=F32,
        )
    low, row, col = lane_masks()
    zero = jnp.zeros((16, LANES), F32)
    for group in range(2):

        def term(along_x, along_y, along_z, column):
            if column < 0 or column >= COLUMNS:
                return zero
            start = tap_index(along_x, along_y, along_z) * OUTS + group * 16
            return z_ref[start : start + 16, column * LANES : (column + 1) * LANES]

        grads = []
        for column in range(COLUMNS):
            total = None
            for c in range(3):
                over_y = None
                for b in range(3):
                    mixed = jnp.where(
                        low,
                        term(2, b, c, column + 1) + term(0, b, c, column),
                        term(2, b, c, column) + term(0, b, c, column - 1),
                    )
                    over_x = term(1, b, c, column) + turn(mixed, 64)
                    if b != 1:
                        over_x = jnp.where(inside(row, b - 1), turn(over_x, -8 * (b - 1)), 0.0)
                    over_y = over_x if over_y is None else over_y + over_x
                if c != 1:
                    over_y = jnp.where(inside(col, c - 1), turn(over_y, -(c - 1)), 0.0)
                total = over_y if total is None else total + over_y
            slab, part = column // 2, column % 2
            lanes = slice(part * LANES, (part + 1) * LANES)
            logistic = 1.0 / (1.0 + jnp.exp(-total))
            out_ref[slab, CELLS + group * 16 : CELLS + group * 16 + 16, lanes] = (
                total * logistic
            ).astype(BF16)
            upstream = r_ref[
                slab, CELLS + group * 16 : CELLS + group * 16 + 16, lanes
            ].astype(F32)
            grad = upstream * (logistic * (1.0 + total * (1.0 - logistic)))
            grads.append(grad.astype(BF16).astype(F32))
        for c in range(3):
            if c == 1:
                by_z = grads
            else:
                by_z = [jnp.where(inside(col, 1 - c), turn(g, c - 1), 0.0) for g in grads]
            for b in range(3):
                if b == 1:
                    by_y = by_z
                else:
                    by_y = [
                        jnp.where(inside(row, 1 - b), turn(g, 8 * (b - 1)), 0.0) for g in by_z
                    ]
                swapped = [zero] + [turn(g, 64) for g in by_y] + [zero]
                for column in range(COLUMNS):
                    lanes = slice(column * LANES, (column + 1) * LANES)
                    here = swapped[column + 1]
                    for a, value in (
                        (0, jnp.where(low, here, swapped[column + 2])),
                        (1, by_y[column]),
                        (2, jnp.where(low, swapped[column], here)),
                    ):
                        start = tap_index(a, b, c) * OUTS + group * 16
                        g_ref[start : start + 16, lanes] = value.astype(BF16)
    whole = jnp.dot(
        g_ref[: TAPS * OUTS, :],
        r_ref[:, :CELLS, :].reshape(WHOLE, CELLS),
        preferred_element_type=F32,
    )
    for tap in range(TAPS):
        start = tap * OUTS
        left = whole[start : start + 16]
        right = whole[start + 16 : start + 32]
        own_ref[tap * 16 : tap * 16 + 16, :] = jnp.where(first, left, right)
        other_ref[tap * 16 : tap * 16 + 16, :] = jnp.where(first, right, left).astype(BF16)
    turned = jnp.transpose(w2_ref[...].astype(F32)).astype(BF16)
    for slab in range(SLABS):
        out_ref[slab, :CELLS, :] = jnp.dot(
            turned, g_ref[:, slab * CELLS : (slab + 1) * CELLS], preferred_element_type=F32
        ).astype(BF16)


def add_kernel(own_ref, got_ref, out_ref):
    out_ref[...] = (own_ref[...] + got_ref[...].astype(F32)).astype(BF16)


def lengthen_kernel(rows_ref, after_ref, out_ref):
    out_ref[: TAPS * 16, :] = rows_ref[...]
    out_ref[TAPS * 16 :, :] = jnp.zeros((out_ref.shape[0] - TAPS * 16, CELLS), BF16)


def share_kernel(parts_ref, out_ref):
    total = parts_ref[0].astype(F32)
    for place in range(1, parts_ref.shape[0]):
        total = total + parts_ref[place].astype(F32)
    for place in range(out_ref.shape[0]):
        out_ref[place] = total.astype(BF16)


def final_kernel(chip_ref, r_ref, act_ref, grad_ref):
    total = r_ref[0, :CELLS, :].astype(F32)
    for slab in range(1, SLABS):
        total = total + r_ref[slab, :CELLS, :].astype(F32)
    grad_ref[...] = jnp.transpose(total).astype(BF16)
    for half in range(2):
        turned = jnp.transpose(
            jnp.concatenate(
                [
                    r_ref[
                        home(pair, core, chip_ref[0]),
                        CELLS + core * 16 : CELLS + core * 16 + 16,
                        :,
                    ].astype(F32)
                    for pair in range(half * 4, half * 4 + 4)
                    for core in range(2)
                ],
                axis=0,
            )
        )
        act_ref[:, half * LANES : (half + 1) * LANES] = turned.astype(BF16)


VMEM = pl.BlockSpec(memory_space=pltpu.VMEM)
SMEM = pl.BlockSpec(memory_space=pltpu.SMEM)
ANY = pl.BlockSpec(memory_space=pl.ANY)
HBM = pl.BlockSpec(memory_space=pltpu.HBM)


def shape(*dims, dtype=BF16):
    return jax.ShapeDtypeStruct(dims, dtype)


def call(kernel, outs, operands, specs=None, scratch=(), flops=0, out_spec=VMEM, vmem=48):
    moved = sum(a.size * a.dtype.itemsize for a in list(operands) + list(outs))
    return pl.pallas_call(
        kernel,
        out_shape=tuple(outs),
        in_specs=specs or [VMEM] * len(operands),
        out_specs=tuple(out_spec for _ in outs),
        scratch_shapes=list(scratch),
        compiler_params=pltpu.CompilerParams(vmem_limit_bytes=vmem * 1024 * 1024),
        cost_estimate=pl.CostEstimate(flops=flops, bytes_accessed=moved, transcendentals=0),
    )(*operands)


def local(inputs, weights, upstream):
    owner = lax.axis_index("fsdp")
    core = (owner % 2).astype(jnp.int32).reshape(1)
    chip = (owner // 2).astype(jnp.int32).reshape(1)
    chips = lax.axis_size("fsdp") // 2
    reps = lax.axis_size("rep")
    total_cells = 2 * chips * reps * WHOLE
    factor = float(total_cells) ** (-0.5)

    def place(z, core, y, rep):
        return ((z * 2 + core) * SLABS + y) * reps + rep

    everyone = ("fsdp", "slab", "rep")
    mirrored = [
        (place(z, core, y, rep), place((y + 4 * core - z) % SLABS, core, y, rep))
        for z in range(chips)
        for core in range(2)
        for y in range(SLABS)
        for rep in range(reps)
    ]
    cores = [(2 * z + core, 2 * z + 1 - core) for z in range(chips) for core in range(2)]

    by_tap = jnp.transpose(weights, (1, 0, 2))
    same = lax.ppermute(by_tap, everyone, mirrored)
    opposite = lax.ppermute(same, "fsdp", cores)

    cells = inputs.reshape(CELLS, CELLS)
    packed = call(
        pack_kernel,
        [shape(SLABS, CELLS + OUTS, CELLS)],
        (chip, cells, upstream.reshape(CELLS, CELLS)),
        specs=[SMEM, HBM, HBM],
        scratch=[
            pltpu.VMEM((CELLS, CELLS), BF16),
            pltpu.VMEM((CELLS, CELLS), BF16),
            pltpu.VMEM((SLABS, OUTS, CELLS), BF16),
            pltpu.SemaphoreType.DMA((4 + 2 * SLABS,)),
        ],
        out_spec=HBM,
        vmem=56,
    )[0]
    gathered = lax.all_to_all(packed, "slab", 0, 0)

    terms, own, other = call(
        main_kernel,
        [
            shape(SLABS, CELLS + OUTS, CELLS),
            shape(TAPS * 16, CELLS, dtype=F32),
            shape(TAPS * 16, CELLS),
        ],
        (core, gathered, same, opposite),
        specs=[SMEM, VMEM, VMEM, VMEM],
        scratch=[
            pltpu.VMEM((ROWS, WHOLE), BF16),
            pltpu.VMEM((ROWS, CELLS), BF16),
            pltpu.VMEM((TAPS * OUTS, WHOLE), F32),
        ],
        flops=6 * ROWS * WHOLE * CELLS,
    )
    returned = lax.all_to_all(terms, "slab", 0, 0)
    activated, input_grad = call(
        final_kernel,
        [shape(CELLS, CELLS), shape(CELLS, CELLS)],
        (chip, returned),
        specs=[SMEM, VMEM],
    )

    sums = call(
        add_kernel,
        [shape(TAPS * 16, CELLS)],
        (own, lax.ppermute(other, "fsdp", cores)),
        flops=AHEAD,
    )[0]
    sums = lax.ppermute(sums, everyone, mirrored)
    plane = SLABS * reps
    sums = call(
        lengthen_kernel,
        [shape(512, CELLS)],
        (sums, returned),
        specs=[VMEM, ANY],
    )[0]
    scattered = lax.all_to_all(
        sums.reshape(plane, 512 // plane, CELLS), ("slab", "rep"), 0, 0
    )
    share = call(share_kernel, [shape(plane, 512 // plane, CELLS)], (scattered,))[0]
    parts = lax.all_to_all(share, ("slab", "rep"), 0, 0).astype(F32)
    weight_grad = jnp.transpose(parts.reshape(32, 16, CELLS)[:TAPS], (1, 0, 2)) * factor
    return (
        activated.reshape(inputs.shape),
        input_grad.reshape(inputs.shape),
        weight_grad,
    )


def solution(mesh):
    placed = (
        P(("fsdp", "rep"), "slab", None, None, None),
        P("fsdp", None, None),
        P(("fsdp", "rep"), "slab", None, None, None),
    )
    return jax.shard_map(
        local,
        mesh=mesh,
        in_specs=placed,
        out_specs=(
            P(("fsdp", "rep"), "slab", None, None, None),
            P(("fsdp", "rep"), "slab", None, None, None),
            P("fsdp", None, None),
        ),
        check_vma=False,
    )
```
